256 devices in a mesh: ao: 16 (over x_hi, z), pair: 16 (over y, x_lo, core).
Axes of the slice: x: 4 (x_hi: 2, x_lo: 2; x = x_hi * 2 + x_lo), y: 4, z: 8, core: 2. Of those that a mesh axis runs over, the one named last changes fastest.
Arguments:
- green_occ: bfloat16 [2048, 2048], P(None, 'ao'), may hold values from -0.75 to 0.75
- green_virtual: bfloat16 [2048, 2048], P(None, 'ao'), may hold values from -0.75 to 0.75
- tile_values: bfloat16 [4096, 64, 128], P(('ao', 'pair')), may hold values from -0.4375 to 0.4375
- tile_orbital: int32 [4096], P(('ao', 'pair')), may hold values from 0 to 31
- tile_window: int32 [4096], P(('ao', 'pair')), may hold values from 0 to 15
- tile_count: int32 [256], P(('ao', 'pair')), may hold values from 1 to 16, as said below
Outputs:
- polarizability: float32 [8192, 1536], P(('ao', 'pair'))
The draws below stay inside these ranges and needn't reach their ends.
Inputs may be any that keep to these rules, and one draw needn't show every extreme that they name: `tile_count`: some row group in every draw has all 16 slots live.
All inputs are finite; a program needn't handle non-finite values.
Results may differ from the reference program's by a relative error of at most 0.0041.
Values may be sent and summed in bfloat16 or wider, within the bound.
No kernel may reach another device: no remote copies, remote signals or barrier semaphores. Data moves between devices by JAX's collectives and lax.ppermute only.
A program may use at most 64 MiB of HBM per device.

```python
import jax
import jax.numpy as jnp
from jax import lax

BLK = 64
CB = 2
LAM_ROWS = 2
RHB = 8
TILES = 16
NAO = 2048
RH = 512
RW = 1024
NRI = 8192
ROW_GROUPS = 256
N_AO = 16
N_PAIR = 16


def draw_tile_count(key, part):
    key = jax.random.fold_in(key, 7)
    first_key, second_key = jax.random.split(key)
    devices_all = N_AO * N_PAIR
    lowest = max(TILES // 4, 1)
    highest = TILES // 2 + 2
    baseline = jax.random.randint(first_key, (devices_all,), lowest, highest)
    centre = jax.random.randint(second_key, (), 0, devices_all)
    nearby = jnp.mod(jnp.arange(devices_all) - centre, devices_all) < max(devices_all // 16, 1)
    return jnp.where(nearby, TILES, baseline).astype(jnp.int32)


def with_ends(result, stream_key, least, largest):
    longest = result.shape.index(max(result.shape))
    spots = []
    for shift in (0, 1):
        where = [jax.random.randint(jax.random.fold_in(stream_key, axis), (), 0, length) for axis, length in enumerate(result.shape)]
        where[longest] = (where[longest] + shift) % result.shape[longest]
        spots.append(tuple(where))
    return result.at[spots[0]].set(least).at[spots[1]].set(largest)


def block_scale(stream_key, dims, shards, low, top_value):
    gain = 1.0
    for position, blocks in shards:
        steps = jax.random.uniform(jax.random.fold_in(jax.random.fold_in(stream_key, 6), position), (blocks,), jnp.float32, low / len(shards), top_value / len(shards))
        gain = gain * jnp.repeat(jnp.exp(steps), dims[position] // blocks).reshape((-1,) + (1,) * (len(dims) - 1 - position))
    return gain


def bell_draw(key, shape, width, reach, cuts=(), kind=jnp.bfloat16):
    values = width * jax.random.normal(key, shape, jnp.float32)
    if cuts:
        values = values * block_scale(key, shape, cuts, -0.22, 0.18)
    return jnp.clip(values, -reach, reach).astype(kind)


def setup_inputs(seed: int = 0) -> dict:
    key_of = jax.random.split(jax.random.key(seed), 7)
    return {
        "green_occ": bell_draw(key_of[0], (NAO, NAO), BLK ** -0.5, 0.75, ((1, 16),)),
        "green_virtual": bell_draw(key_of[1], (NAO, NAO), BLK ** -0.5, 0.75, ((1, 16),)),
        "tile_values": bell_draw(key_of[2], (ROW_GROUPS * TILES, BLK, LAM_ROWS * BLK), 0.07, 0.4375, ((0, 256),)),
        "tile_orbital": with_ends(jax.random.randint(key_of[3], (ROW_GROUPS * TILES,), 0, N_AO * CB), jax.random.fold_in(key_of[3], 1), 0, (N_AO * CB) - 1).astype(jnp.int32),
        "tile_window": with_ends(jax.random.randint(key_of[4], (ROW_GROUPS * TILES,), 0, 2 * RHB), jax.random.fold_in(key_of[4], 1), 0, (2 * RHB) - 1).astype(jnp.int32),
        "tile_count": draw_tile_count(jax.random.fold_in(key_of[6], 71), 0),
    }


def moments(green_blocks, tile_block, orbital_block, onehot):
    picked_rows = green_blocks[orbital_block]
    product = jnp.einsum("cjs,cjx->csx", picked_rows.astype(jnp.float32), tile_block.astype(jnp.float32), precision=lax.Precision.HIGHEST)
    product = product.reshape(TILES, NAO, LAM_ROWS, BLK)
    moment = jnp.einsum("csiq,cr->sirq", product, onehot, precision=lax.Precision.HIGHEST)
    return moment.reshape(NAO * LAM_ROWS, RW).astype(jnp.bfloat16)


def reference(green_occ, green_virtual, tile_values, tile_orbital, tile_window, tile_count):
    occ_blocks = green_occ.reshape(NAO // BLK, BLK, NAO)
    vir_blocks = green_virtual.reshape(NAO // BLK, BLK, NAO)
    values_all = tile_values.reshape(N_AO, N_PAIR, TILES, BLK, LAM_ROWS * BLK)
    orbital_all = tile_orbital.reshape(N_AO, N_PAIR, TILES)
    window_all = tile_window.reshape(N_AO, N_PAIR, TILES)
    counts_all = tile_count.reshape(N_AO, N_PAIR)

    def group_window(item):
        def member(running_sum, inner):
            tile_block, orbital_block, window_block, live_count = inner
            live_slots = jnp.arange(TILES, dtype=jnp.int32) < live_count
            targets = jnp.arange(2 * RHB, dtype=jnp.int32)
            onehot = ((window_block[:, None] == targets[None, :]) & live_slots[:, None]).astype(jnp.float32)
            occ_moment = moments(occ_blocks, tile_block, orbital_block, onehot)
            vir_moment = moments(vir_blocks, tile_block, orbital_block, onehot)
            product = lax.dot_general(occ_moment, vir_moment, (((0,), (0,)), ((), ())), preferred_element_type=jnp.float32)
            return running_sum + product, None

        running_sum, unused = lax.scan(member, jnp.zeros((RW, RW), jnp.float32), item)
        return running_sum

    windows = lax.map(group_window, (values_all, orbital_all, window_all, counts_all))
    upper_band = windows[:, :RH, :]
    lower_band = jnp.roll(windows[:, RH:, :], 1, axis=0)
    band = jnp.concatenate([lower_band[:, :, :RH], lower_band[:, :, RH:] + upper_band[:, :, :RH], upper_band[:, :, RH:]], axis=2)
    return band.reshape(NRI, 3 * RH)
```

```python
import functools

import jax
import jax.numpy as jnp
from jax import lax
from jax.experimental import pallas as pl
from jax.experimental.pallas import tpu as pltpu
from jax.sharding import PartitionSpec as P

AXES = ("ao", "pair")
BLK = 64
TILES = 16
PAIRS = TILES // 2
NAO = 2048
RW = 1024
COLS = 128
PIECE = NAO // 8
META = 16
BODY = PAIRS * 128
PAY = BODY + META
GROUPS = 8
DEPTH = GROUPS * 512
BF = jnp.bfloat16
F32 = jnp.float32


def device_of(index):
    ao, pair = index // 16, index % 16
    return ao // 8, ao % 8, pair // 4, (pair // 2) % 2, pair % 2


def index_of(x_hi, z, y, x_lo, core):
    return ((x_hi % 2) * 8 + z % 8) * 16 + ((y % 4) * 2 + x_lo % 2) * 2 + core % 2


def permute(value, where):
    pairs = [(source, index_of(*where(*device_of(source)))) for source in range(256)]
    return lax.ppermute(value, AXES, pairs)


def along_y(value, steps):
    return permute(value, lambda x_hi, z, y, x_lo, core: (x_hi, z, y + steps, x_lo, core))


def along_z(value, steps):
    return permute(value, lambda x_hi, z, y, x_lo, core: (x_hi, z + steps, y, x_lo, core))


def swap_x(value):
    return permute(value, lambda x_hi, z, y, x_lo, core: (x_hi, z, y, x_lo + 1, core))


def swap_core(value):
    return permute(value, lambda x_hi, z, y, x_lo, core: (x_hi, z, y, x_lo, core + 1))


def next_group(value, flip):
    def where(x_hi, z, y, x_lo, core):
        return (x_hi + (z == 7), z + 1, y, x_lo + flip, core)

    return permute(value, where)


Z_OFFSETS = ((3, 4), (1, 2), (0, 7), (5, 6))


def scatter_target(x_hi, z, y, x_lo, core):
    block = x_hi * 8 + z
    target_y, target_x, target_core = block // 4, (block // 2) % 2, block % 2
    target_hi = x_hi if x_lo == target_x else 1 - x_hi
    offset = Z_OFFSETS[(y - target_y) % 4][core]
    return target_hi, z + offset, target_y, target_x, target_core


def scatter_green(green_occ, green_virtual):
    table = jnp.array([scatter_target(*device_of(index))[1] % 8 for index in range(256)], jnp.int32)
    me = lax.axis_index("ao") * 16 + lax.axis_index("pair")
    start = table[me] * PIECE
    both = jnp.concatenate(
        [lax.dynamic_slice_in_dim(part, start, PIECE, 0) for part in (green_occ, green_virtual)], axis=1
    )
    return permute(both, scatter_target)


def pack_kernel(orbital_ref, window_ref, count_ref, tile_ref, out_ref, order_ref):
    live = count_ref[0]
    windows = [window_ref[slot] for slot in range(TILES)]
    keys = [
        jnp.where(slot < live, windows[slot], TILES) * TILES + slot for slot in range(TILES)
    ]
    ranks = [jnp.int32(0) for slot in range(TILES)]
    for first in range(TILES):
        for second in range(first + 1, TILES):
            later = (keys[second] < keys[first]).astype(jnp.int32)
            ranks[first] = ranks[first] + later
            ranks[second] = ranks[second] + (1 - later)
    for slot in range(TILES):
        order_ref[ranks[slot]] = slot
    lane = lax.broadcasted_iota(jnp.int32, (META, 128), 1)
    meta = jnp.where(lane == 32, live, jnp.zeros((META, 128), jnp.int32))
    last = jnp.int32(0)
    for slot in range(TILES):
        source = order_ref[slot]
        last = jnp.where(slot < live, window_ref[source], last)
        meta = jnp.where(lane == slot, last, meta)
        meta = jnp.where(lane == TILES + slot, orbital_ref[source], meta)
    for index in range(PAIRS):
        rows = []
        for slot in (2 * index, 2 * index + 1):
            rows.append(jnp.where(slot < live, tile_ref[order_ref[slot]].astype(F32), 0.0))
        both = jnp.concatenate(rows, axis=0)
        out_ref[pl.ds(index * 128, 128), :] = both.T.astype(BF)
    out_ref[pl.ds(BODY, META), :] = meta.astype(F32).astype(BF)


def pack(tile_orbital, tile_window, tile_count, tile_values):
    smem = pl.BlockSpec(memory_space=pltpu.SMEM)
    return pl.pallas_call(
        pack_kernel,
        out_shape=jax.ShapeDtypeStruct((PAY, 128), BF),
        in_specs=[smem, smem, smem, pl.BlockSpec(memory_space=pltpu.VMEM)],
        out_specs=pl.BlockSpec(memory_space=pltpu.VMEM),
        scratch_shapes=[pltpu.SMEM((TILES,), jnp.int32)],
    )(tile_orbital, tile_window, tile_count, tile_values)


def chi_kernel(
    place_ref, meta_ref, own_ref, east_ref, west_ref, far_a_ref, far_b_ref,
    green_ref, other_ref, keep_ref, send_ref, occ_ref, vir_ref, acc_ref,
):
    my_z, my_y, my_x, my_core = place_ref[0], place_ref[1], place_ref[2], place_ref[3]
    occ_ref[...] = jnp.zeros_like(occ_ref)
    vir_ref[...] = jnp.zeros_like(vir_ref)
    lane = lax.broadcasted_iota(jnp.int32, (128, 128), 1)

    def rows_of(orbital):
        piece = lax.rem(orbital // 4 - my_z + 8, 8)
        start = pl.multiple_of(piece * PIECE + lax.rem(orbital, 4) * BLK, BLK)
        return jnp.concatenate(
            [green_ref[pl.ds(start, BLK), :], other_ref[pl.ds(start, BLK), :]], axis=1
        )

    def group(tiles_ref, base, number):
        live = meta_ref[number, 2 * TILES]
        column = number * 512

        def step(index, carry):
            first, second = 2 * index, 2 * index + 1
            tile = tiles_ref[pl.ds(pl.multiple_of(base + index * 128, 16), 128), :]
            zero = jnp.zeros_like(tile)
            stacked = jnp.concatenate(
                [jnp.where(lane < BLK, tile, zero), jnp.where(lane < BLK, zero, tile)], axis=0
            )
            rows = jnp.concatenate(
                [rows_of(meta_ref[number, TILES + first]), rows_of(meta_ref[number, TILES + second])], axis=0
            )
            product = jnp.dot(stacked, rows, preferred_element_type=F32)
            windows = [meta_ref[number, first], meta_ref[number, second]]
            before = jnp.where(index > 0, meta_ref[number, jnp.maximum(first - 1, 0)], -1)
            total = product[:128]
            total = jnp.where(windows[0] == before, acc_ref[...] + total, total)
            store(total, windows[0])
            total = jnp.where(windows[1] == windows[0], total + product[128:], product[128:])
            acc_ref[...] = total
            store(total, windows[1])
            return carry

        def store(total, window):
            high, y, x = window // 8, lax.rem(window // 2, 4), lax.rem(window, 2)
            dy, dx = lax.rem(y - my_y + 4, 4), lax.rem(x - my_x + 2, 2)
            spot = ((dy * 2 + dx) * 2 + high) * 32
            vir_row = pl.multiple_of(window * BLK, BLK)
            half = total.astype(BF)
            for i in range(2):
                part = half[i * BLK:(i + 1) * BLK]
                occ = jnp.concatenate([part[:, 0:128], part[:, 256:384]], axis=1)
                vir = jnp.concatenate([part[:, 128:256], part[:, 384:512]], axis=1)
                vir_ref[pl.ds(vir_row, BLK), pl.ds(column + i * 256, 256)] = vir
                for core in range(2):
                    row = jnp.where(my_core == core, 0, 512) + spot
                    row = pl.multiple_of(row, 32)
                    occ_ref[pl.ds(row, 32), pl.ds(column + i * 256, 256)] = occ[core * 32:(core + 1) * 32]

        lax.fori_loop(0, lax.div(live + 1, 2), step, 0)

    number = 0
    for tiles_ref in (own_ref, east_ref, west_ref, far_a_ref, far_b_ref):
        for base in range(0, tiles_ref.shape[0], PAY):
            group(tiles_ref, base, number)
            number += 1

    def chi(row, target_ref, kind):
        for m in range(0, 512, 256):
            @pl.loop(0, RW, step=256)
            def _(n):
                n = pl.multiple_of(n, 256)
                product = lax.dot_general(
                    occ_ref[pl.ds(row + m, 256), :], vir_ref[pl.ds(n, 256), :],
                    (((1,), (1,)), ((), ())), preferred_element_type=F32,
                )
                target_ref[pl.ds(m, 256), pl.ds(n, 256)] = product.astype(kind)

    chi(512, send_ref, BF)
    chi(0, keep_ref, F32)


def chi_call(place, meta, tiles, green, other):
    smem = pl.BlockSpec(memory_space=pltpu.SMEM)
    vmem = pl.BlockSpec(memory_space=pltpu.VMEM)
    return pl.pallas_call(
        chi_kernel,
        out_shape=(jax.ShapeDtypeStruct((512, RW), F32), jax.ShapeDtypeStruct((512, RW), BF)),
        in_specs=[smem, smem] + [vmem] * 7,
        out_specs=(vmem, vmem),
        scratch_shapes=[
            pltpu.VMEM((RW, DEPTH), BF),
            pltpu.VMEM((RW, DEPTH), BF),
            pltpu.VMEM((128, 512), F32),
        ],
        compiler_params=pltpu.CompilerParams(vmem_limit_bytes=48 * 1024 * 1024),
        cost_estimate=pl.CostEstimate(flops=12 * 10**9, bytes_accessed=8 * 2**20, transcendentals=0),
    )(place, meta, *tiles, green, other)


def gather_tiles(payload):
    own = jnp.concatenate([payload, swap_x(payload)], axis=0)
    east = along_y(own, 1)
    west = along_y(own, -1)
    far_a = along_y(east[:PAY], 1)
    far_b = along_y(west[PAY:], -1)
    return own, east, west, far_a, far_b


def gather_green(piece):
    up, down = piece, piece
    ups, downs = [], []
    for unused in range(3):
        up = along_z(up, 1)
        down = along_z(down, -1)
        ups.append(up)
        downs.append(down)
    half = PIECE // 2
    across = [along_z(up[:half], 1), along_z(down[half:], -1)]
    return jnp.concatenate([piece] + downs + across + ups[::-1], axis=0)


def reduce_band(keep, send):
    quarters = (keep + swap_core(send).astype(F32)).astype(F32).reshape(4, 128, RW)
    ahead = along_y(quarters[2, :64].astype(BF), 1).astype(F32)
    behind = along_y(quarters[2, 64:].astype(BF), -1).astype(F32)
    up = jnp.concatenate([quarters[1, :64] + ahead, quarters[1, 64:]], axis=0).astype(BF)
    down = jnp.concatenate([quarters[3, :64], quarters[3, 64:] + behind], axis=0).astype(BF)
    total = quarters[0] + along_y(up, 1).astype(F32) + along_y(down, -1).astype(F32)
    upper = total[:32] + swap_x(total[64:96].astype(BF)).astype(F32)
    lower = next_group(total[32:64].astype(BF), 0).astype(F32) + next_group(total[96:].astype(BF), 1).astype(F32)
    return jnp.concatenate([lower[:, :512], lower[:, 512:] + upper[:, :512], upper[:, 512:]], axis=1)


def per_device(green_occ, green_virtual, tile_values, tile_orbital, tile_window, tile_count):
    ao, pair = lax.axis_index("ao"), lax.axis_index("pair")
    place = jnp.stack([ao % 8, pair // 4, (pair // 2) % 2, pair % 2]).astype(jnp.int32)
    piece = scatter_green(green_occ, green_virtual)
    payload = pack(tile_orbital, tile_window, tile_count, tile_values)
    tiles = gather_tiles(payload)
    green = gather_green(piece)
    other = swap_core(green)
    rows = [part[start + BODY:start + BODY + 1, :64] for part in tiles for start in range(0, part.shape[0], PAY)]
    meta = jnp.concatenate(rows, axis=0).astype(jnp.int32)
    keep, send = chi_call(place, meta, tiles, green, other)
    return reduce_band(keep, send)


def solution(mesh):
    in_specs = (
        P(None, "ao"),
        P(None, "ao"),
        P(("ao", "pair"), None, None),
        P(("ao", "pair")),
        P(("ao", "pair")),
        P(("ao", "pair")),
    )
    out_specs = P(("ao", "pair"), None)
    return jax.shard_map(
        per_device, mesh=mesh, in_specs=in_specs, out_specs=out_specs, check_vma=False
    )
```

```python
import functools

import jax
import jax.numpy as jnp
from jax import lax
from jax.experimental import pallas as pl
from jax.experimental.pallas import tpu as pltpu
from jax.sharding import PartitionSpec as P

AXES = ("ao", "pair")
BLK = 64
TILES = 16
PAIRS = TILES // 2
NAO = 2048
RW = 1024
COLS = 128
PIECE = NAO // 8
META = 16
BODY = PAIRS * 128
PAY = BODY + META
GROUPS = 8
DEPTH = GROUPS * 512
BF = jnp.bfloat16
F32 = jnp.float32


def device_of(index):
    ao, pair = index // 16, index % 16
    return ao // 8, ao % 8, pair // 4, (pair // 2) % 2, pair % 2


def index_of(x_hi, z, y, x_lo, core):
    return ((x_hi % 2) * 8 + z % 8) * 16 + ((y % 4) * 2 + x_lo % 2) * 2 + core % 2


def permute(value, where):
    pairs = [(source, index_of(*where(*device_of(source)))) for source in range(256)]
    return lax.ppermute(value, AXES, pairs)


def along_y(value, steps):
    return permute(value, lambda x_hi, z, y, x_lo, core: (x_hi, z, y + steps, x_lo, core))


def along_z(value, steps):
    return permute(value, lambda x_hi, z, y, x_lo, core: (x_hi, z + steps, y, x_lo, core))


def swap_x(value):
    return permute(value, lambda x_hi, z, y, x_lo, core: (x_hi, z, y, x_lo + 1, core))


def swap_core(value):
    return permute(value, lambda x_hi, z, y, x_lo, core: (x_hi, z, y, x_lo, core + 1))


def next_group(value, flip):
    def where(x_hi, z, y, x_lo, core):
        return (x_hi + (z == 7), z + 1, y, x_lo + flip, core)

    return permute(value, where)


def scatter_target(x_hi, z, y, x_lo, core):
    target_y, target_x, target_core = x_hi * 2 + z // 4, (z // 2) % 2, z % 2
    target_hi = x_hi + (x_lo - target_x) % 2
    return target_hi, z + 3 - 2 * ((y - target_y) % 4) + core, target_y, target_x, target_core


def scatter_pieces(green_occ, green_virtual, x_hi, z, y, core):
    target_z = (z + 11 - 2 * ((y - x_hi * 2 - z // 4 + 4) % 4) + core) % 8
    both = jnp.concatenate([green_occ, green_virtual], axis=1)
    starts = (target_z * PIECE, (target_z + 4) % 8 * PIECE)
    return jnp.concatenate([lax.dynamic_slice_in_dim(both, start, PIECE, 0) for start in starts], axis=0)


def pack_kernel(orbital_ref, window_ref, count_ref, tile_ref, out_ref, order_ref):
    live = count_ref[0]
    windows = [window_ref[slot] for slot in range(TILES)]
    keys = [
        jnp.where(slot < live, windows[slot], TILES) * TILES + slot for slot in range(TILES)
    ]
    ranks = [jnp.int32(0) for slot in range(TILES)]
    for first in range(TILES):
        for second in range(first + 1, TILES):
            later = (keys[second] < keys[first]).astype(jnp.int32)
            ranks[first] = ranks[first] + later
            ranks[second] = ranks[second] + (1 - later)
    for slot in range(TILES):
        order_ref[ranks[slot]] = slot
    lane = lax.broadcasted_iota(jnp.int32, (META, 128), 1)
    meta = jnp.where(lane == 32, live, jnp.zeros((META, 128), jnp.int32))
    last = jnp.int32(0)
    for slot in range(TILES):
        source = order_ref[slot]
        last = jnp.where(slot < live, window_ref[source], last)
        meta = jnp.where(lane == slot, last, meta)
        meta = jnp.where(lane == TILES + slot, orbital_ref[source], meta)
    for index in range(PAIRS):
        rows = []
        for slot in (2 * index, 2 * index + 1):
            rows.append(jnp.where(slot < live, tile_ref[order_ref[slot]].astype(F32), 0.0))
        both = jnp.concatenate(rows, axis=0)
        out_ref[pl.ds(index * 128, 128), :] = both.T.astype(BF)
    out_ref[pl.ds(BODY, META), :] = meta.astype(F32).astype(BF)


def pack(tile_orbital, tile_window, tile_count, tile_values):
    smem = pl.BlockSpec(memory_space=pltpu.SMEM)
    return pl.pallas_call(
        pack_kernel,
        out_shape=jax.ShapeDtypeStruct((PAY, 128), BF),
        in_specs=[smem, smem, smem, pl.BlockSpec(memory_space=pltpu.VMEM)],
        out_specs=pl.BlockSpec(memory_space=pltpu.VMEM),
        scratch_shapes=[pltpu.SMEM((TILES,), jnp.int32)],
    )(tile_orbital, tile_window, tile_count, tile_values)


def chi_kernel(
    place_ref, meta_ref, own_ref, east_ref, west_ref, far_a_ref, far_b_ref,
    green_ref, other_ref, keep0_ref, keep1_ref, keep2_ref, keep3_ref, send_ref, occ_ref, vir_ref, acc_ref,
):
    keep_refs = (keep0_ref, keep1_ref, keep2_ref, keep3_ref)
    my_z, my_y, my_x, my_core = place_ref[0], place_ref[1], place_ref[2], place_ref[3]
    occ_ref[...] = jnp.zeros_like(occ_ref)
    vir_ref[...] = jnp.zeros_like(vir_ref)
    def rows_of(orbital):
        piece = lax.rem(orbital // 4 - my_z + 8, 8)
        start = pl.multiple_of(piece * PIECE + lax.rem(orbital, 4) * BLK, BLK)
        return jnp.concatenate(
            [green_ref[pl.ds(start, BLK), :], other_ref[pl.ds(start, BLK), :]], axis=1
        )

    def store(block, window, column):
        high, y, x = window // 8, lax.rem(window // 2, 4), lax.rem(window, 2)
        dy, dx = lax.rem(y - my_y + 4, 4), lax.rem(x - my_x + 2, 2)
        spot = ((dy * 2 + dx) * 2 + high) * 32
        vir_row = pl.multiple_of(window * BLK, BLK)
        for i in range(2):
            part = block[i * BLK:(i + 1) * BLK]
            occ = jnp.concatenate([part[:, 0:128], part[:, 256:384]], axis=1)
            vir = jnp.concatenate([part[:, 128:256], part[:, 384:512]], axis=1)
            vir_ref[pl.ds(vir_row, BLK), pl.ds(column + i * 256, 256)] = vir
            for core in range(2):
                row = pl.multiple_of(jnp.where(my_core == core, 0, 512) + spot, 32)
                occ_ref[pl.ds(row, 32), pl.ds(column + i * 256, 256)] = occ[core * 32:(core + 1) * 32]

    lane = lax.broadcasted_iota(jnp.int32, (128, 128), 1) // BLK

    def group(tiles_ref, base, number):
        live = meta_ref[number, 2 * TILES]
        column = number * 512

        def step(index, carry):
            slots = [4 * index + t for t in range(4)]
            windows = [meta_ref[number, slot] for slot in slots]
            before = jnp.where(index > 0, meta_ref[number, jnp.maximum(slots[0] - 1, 0)], -1)
            halves = [
                tiles_ref[pl.ds(pl.multiple_of(base + index * 256 + k * 128, 16), 128), :]
                for k in range(2)
            ]
            zero = jnp.zeros_like(halves[0])
            stacked = []
            for t in range(4):
                parts = []
                for k in range(2):
                    even = (2 * k <= t) & (windows[min(2 * k, t)] == windows[t])
                    odd = (2 * k + 1 <= t) & (windows[min(2 * k + 1, t)] == windows[t])
                    if 2 * k > t:
                        parts.append(zero)
                    else:
                        keep = jnp.where(lane == 0, even.astype(jnp.int32) if not isinstance(even, bool) else int(even), odd.astype(jnp.int32) if not isinstance(odd, bool) else int(odd))
                        parts.append(jnp.where(keep > 0, halves[k], zero))
                stacked.append(jnp.concatenate(parts, axis=1))
            stacked = jnp.concatenate(stacked, axis=0)
            rows = jnp.concatenate([rows_of(meta_ref[number, TILES + slot]) for slot in slots], axis=0)

            def finish(product):
                acc_ref[...] = product[384:]
                half = product.astype(BF)
                for t in range(4):
                    store(half[t * 128:(t + 1) * 128], windows[t], column)

            @pl.when(windows[0] != before)
            def _():
                finish(jnp.dot(stacked, rows, preferred_element_type=F32))

            @pl.when(windows[0] == before)
            def _():
                product = jnp.dot(stacked, rows, preferred_element_type=F32)
                carried = acc_ref[...]
                finish(jnp.concatenate(
                    [product[t * 128:(t + 1) * 128] + jnp.where(windows[t] == before, carried, 0.0) for t in range(4)],
                    axis=0,
                ))

            return carry

        lax.fori_loop(0, lax.div(live + 3, 4), step, 0)

    number = 0
    for tiles_ref in (own_ref, east_ref, west_ref, far_a_ref, far_b_ref):
        for base in range(0, tiles_ref.shape[0], PAY):
            group(tiles_ref, base, number)
            number += 1

    def chi(row, rows):
        return lax.dot_general(
            occ_ref[pl.ds(row, rows), :], vir_ref[...], (((1,), (1,)), ((), ())), preferred_element_type=F32
        )

    send_ref[...] = chi(512, 512).astype(BF)
    product = chi(0, 512)
    for quarter in range(4):
        keep_refs[quarter][...] = product[quarter * 128:(quarter + 1) * 128]


def chi_call(place, meta, tiles, green, other):
    smem = pl.BlockSpec(memory_space=pltpu.SMEM)
    vmem = pl.BlockSpec(memory_space=pltpu.VMEM)
    return pl.pallas_call(
        chi_kernel,
        out_shape=(jax.ShapeDtypeStruct((128, RW), F32),) * 4 + (jax.ShapeDtypeStruct((512, RW), BF),),
        in_specs=[smem, smem] + [vmem] * 7,
        out_specs=(vmem,) * 5,
        scratch_shapes=[
            pltpu.VMEM((RW, DEPTH), BF),
            pltpu.VMEM((RW, DEPTH), BF),
            pltpu.VMEM((128, 512), F32),
        ],
        compiler_params=pltpu.CompilerParams(vmem_limit_bytes=48 * 1024 * 1024),
        cost_estimate=pl.CostEstimate(flops=12 * 10**9, bytes_accessed=8 * 2**20, transcendentals=0),
    )(place, meta, *tiles, green, other)


def together(*values):
    return lax.optimization_barrier(values)


def gather(payload, pieces):
    payload, pieces = together(payload, pieces)
    first = permute(pieces, scatter_target)
    own = jnp.concatenate([payload, swap_x(payload)], axis=0)
    own, first = together(own, first)
    below, above = along_z(first, 1), along_z(first, -1)
    east, west = along_y(own, 1), along_y(own, -1)
    below, above, east, west = together(below, above, east, west)
    near = swap_core(jnp.concatenate([first, above, below], axis=0))
    two_below, two_above = along_z(below[:PIECE], 1), along_z(above[:PIECE], -1)
    far_a, far_b = along_y(east[:PAY], 1), along_y(west[PAY:], -1)
    two_below, two_above, near = together(two_below, two_above, near)
    rest = swap_core(jnp.concatenate([two_above, two_below], axis=0))
    green = by_offset(first, above, below, two_above, two_below)
    other = by_offset(
        near[:2 * PIECE], near[2 * PIECE:4 * PIECE], near[4 * PIECE:], rest[:PIECE], rest[PIECE:]
    )
    return (own, east, west, far_a, far_b), green, other


def by_offset(first, above, below, two_above, two_below):
    parts = (
        first[:PIECE], above[:PIECE], two_above, below[PIECE:],
        first[PIECE:], above[PIECE:], two_below, below[:PIECE],
    )
    return jnp.concatenate(parts, axis=0)


def reduce_band(keeps, send):
    got = swap_core(send)
    parts = [got[quarter * 128:(quarter + 1) * 128] for quarter in range(4)]
    across = keeps[2] + parts[2].astype(F32)
    ahead = along_y(across[:64].astype(BF), 1)
    behind = along_y(across[64:].astype(BF), -1)
    one, three = keeps[1] + parts[1].astype(F32), keeps[3] + parts[3].astype(F32)
    up = jnp.concatenate([one[:64] + ahead.astype(F32), one[64:]], axis=0).astype(BF)
    down = jnp.concatenate([three[:64], three[64:] + behind.astype(F32)], axis=0).astype(BF)
    up, down = along_y(up, 1), along_y(down, -1)
    total = keeps[0] + parts[0].astype(F32) + up.astype(F32) + down.astype(F32)
    upper = total[:32] + swap_x(total[64:96].astype(BF)).astype(F32)
    lower = next_group(total[32:64].astype(BF), 0).astype(F32) + next_group(total[96:].astype(BF), 1).astype(F32)
    return jnp.concatenate([lower[:, :512], lower[:, 512:] + upper[:, :512], upper[:, 512:]], axis=1)


def per_device(green_occ, green_virtual, tile_values, tile_orbital, tile_window, tile_count):
    ao, pair = lax.axis_index("ao"), lax.axis_index("pair")
    x_hi, z, y, x_lo, core = device_of(ao * 16 + pair)
    place = jnp.stack([z, y, x_lo, core]).astype(jnp.int32)
    pieces = scatter_pieces(green_occ, green_virtual, x_hi, z, y, core)
    payload = pack(tile_orbital, tile_window, tile_count, tile_values)
    tiles, green, other = gather(payload, pieces)
    rows = [part[start + BODY:start + BODY + 1, :64] for part in tiles for start in range(0, part.shape[0], PAY)]
    meta = jnp.concatenate(rows, axis=0).astype(jnp.int32)
    *keeps, send = chi_call(place, meta, tiles, green, other)
    return reduce_band(keeps, send)


def solution(mesh):
    in_specs = (
        P(None, "ao"),
        P(None, "ao"),
        P(("ao", "pair"), None, None),
        P(("ao", "pair")),
        P(("ao", "pair")),
        P(("ao", "pair")),
    )
    out_specs = P(("ao", "pair"), None)
    return jax.shard_map(
        per_device, mesh=mesh, in_specs=in_specs, out_specs=out_specs, check_vma=False
    )
```

```python
import functools

import jax
import jax.numpy as jnp
from jax import lax
from jax.experimental import pallas as pl
from jax.experimental.pallas import tpu as pltpu
from jax.sharding import PartitionSpec as P

AXES = ("ao", "pair")
BLK = 64
TILES = 16
PAIRS = TILES // 2
NAO = 2048
RW = 1024
COLS = 128
PIECE = NAO // 8
META = 16
BODY = PAIRS * 128
PAY = BODY + META
GROUPS = 8
DEPTH = GROUPS * 512
BF = jnp.bfloat16
F32 = jnp.float32


def device_of(index):
    ao, pair = index // 16, index % 16
    return ao // 8, ao % 8, pair // 4, (pair // 2) % 2, pair % 2


def index_of(x_hi, z, y, x_lo, core):
    return ((x_hi % 2) * 8 + z % 8) * 16 + ((y % 4) * 2 + x_lo % 2) * 2 + core % 2


def permute(value, where):
    pairs = [(source, index_of(*where(*device_of(source)))) for source in range(256)]
    return lax.ppermute(value, AXES, pairs)


def along_y(value, steps):
    return permute(value, lambda x_hi, z, y, x_lo, core: (x_hi, z, y + steps, x_lo, core))


def along_z(value, steps):
    return permute(value, lambda x_hi, z, y, x_lo, core: (x_hi, z + steps, y, x_lo, core))


def swap_x(value):
    return permute(value, lambda x_hi, z, y, x_lo, core: (x_hi, z, y, x_lo + 1, core))


def swap_core(value):
    return permute(value, lambda x_hi, z, y, x_lo, core: (x_hi, z, y, x_lo, core + 1))


def next_group(value, flip):
    def where(x_hi, z, y, x_lo, core):
        return (x_hi + (z == 7), z + 1, y, x_lo + flip, core)

    return permute(value, where)


Z_OFFSETS = (3, 6, 1, 5, 7, 0, 4, 2)


def scatter_target(x_hi, z, y, x_lo, core):
    target_y, target_x, target_core = z % 4, x_hi, z // 4
    target_hi = x_hi + (x_lo - target_x) % 2
    return target_hi, z + Z_OFFSETS[(y - target_y) % 4 * 2 + core], target_y, target_x, target_core


def scatter_pieces(green_occ, green_virtual, z, y, core):
    case = (y - z % 4 + 4) % 4 * 2 + core
    target_z = (z + sum(offset * (case == number) for number, offset in enumerate(Z_OFFSETS))) % 8
    both = jnp.concatenate([green_occ, green_virtual], axis=1)
    starts = (target_z * PIECE, (target_z + 4) % 8 * PIECE)
    return jnp.concatenate([lax.dynamic_slice_in_dim(both, start, PIECE, 0) for start in starts], axis=0)


def pack_kernel(orbital_ref, window_ref, count_ref, tile_ref, out_ref, order_ref):
    live = count_ref[0]
    windows = [window_ref[slot] for slot in range(TILES)]
    keys = [
        jnp.where(slot < live, windows[slot], TILES) * TILES + slot for slot in range(TILES)
    ]
    ranks = [jnp.int32(0) for slot in range(TILES)]
    for first in range(TILES):
        for second in range(first + 1, TILES):
            later = (keys[second] < keys[first]).astype(jnp.int32)
            ranks[first] = ranks[first] + later
            ranks[second] = ranks[second] + (1 - later)
    for slot in range(TILES):
        order_ref[ranks[slot]] = slot
    lane = lax.broadcasted_iota(jnp.int32, (META, 128), 1)
    meta = jnp.where(lane == 32, live, jnp.zeros((META, 128), jnp.int32))
    last = jnp.int32(0)
    for slot in range(TILES):
        source = order_ref[slot]
        last = jnp.where(slot < live, window_ref[source], last)
        meta = jnp.where(lane == slot, last, meta)
        meta = jnp.where(lane == TILES + slot, orbital_ref[source], meta)
    for index in range(PAIRS):
        rows = []
        for slot in (2 * index, 2 * index + 1):
            rows.append(jnp.where(slot < live, tile_ref[order_ref[slot]].astype(F32), 0.0))
        both = jnp.concatenate(rows, axis=0)
        out_ref[pl.ds(index * 128, 128), :] = both.T.astype(BF)
    out_ref[pl.ds(BODY, META), :] = meta.astype(F32).astype(BF)


def pack(tile_orbital, tile_window, tile_count, tile_values):
    smem = pl.BlockSpec(memory_space=pltpu.SMEM)
    return pl.pallas_call(
        pack_kernel,
        out_shape=jax.ShapeDtypeStruct((PAY, 128), BF),
        in_specs=[smem, smem, smem, pl.BlockSpec(memory_space=pltpu.VMEM)],
        out_specs=pl.BlockSpec(memory_space=pltpu.VMEM),
        scratch_shapes=[pltpu.SMEM((TILES,), jnp.int32)],
    )(tile_orbital, tile_window, tile_count, tile_values)


def chi_kernel(
    place_ref, meta_ref, own_ref, east_ref, west_ref, far_a_ref, far_b_ref,
    first_ref, above_ref, below_ref, two_above_ref, two_below_ref, near_ref, rest_ref,
    keep0_ref, keep1_ref, keep2_ref, keep3_ref, send_ref, green_ref, occ_ref, vir_ref,
):
    keep_refs = (keep0_ref, keep1_ref, keep2_ref, keep3_ref)
    my_z, my_y, my_x, my_core = place_ref[0], place_ref[1], place_ref[2], place_ref[3]
    occ_ref[...] = jnp.zeros_like(occ_ref)
    vir_ref[...] = jnp.zeros_like(vir_ref)

    own_parts = (
        (first_ref, 0, 0), (first_ref, 1, 4), (above_ref, 0, 1), (above_ref, 1, 5),
        (below_ref, 0, 7), (below_ref, 1, 3), (two_above_ref, 0, 2), (two_below_ref, 0, 6),
    )
    other_parts = (
        (near_ref, 0, 0), (near_ref, 1, 4), (near_ref, 2, 1), (near_ref, 3, 5),
        (near_ref, 4, 7), (near_ref, 5, 3), (rest_ref, 0, 2), (rest_ref, 1, 6),
    )
    for lanes, parts in ((0, own_parts), (256, other_parts)):
        for ref, spot, offset in parts:
            start = pl.multiple_of(lax.rem(my_z + offset, 8) * PIECE, PIECE)
            green_ref[pl.ds(start, PIECE), lanes:lanes + 256] = ref[spot * PIECE:(spot + 1) * PIECE, :]

    def rows_of(orbital):
        return green_ref[pl.ds(pl.multiple_of(orbital * BLK, BLK), BLK), :]

    def store(block, window, column):
        high, y, x = window // 8, lax.rem(window // 2, 4), lax.rem(window, 2)
        dy, dx = lax.rem(y - my_y + 4, 4), lax.rem(x - my_x + 2, 2)
        spot = ((dy * 2 + dx) * 2 + high) * 32
        vir_row = pl.multiple_of(window * BLK, BLK)
        for i in range(2):
            part = block[i * BLK:(i + 1) * BLK]
            occ = jnp.concatenate([part[:, 0:128], part[:, 256:384]], axis=1)
            vir = jnp.concatenate([part[:, 128:256], part[:, 384:512]], axis=1)
            vir_ref[pl.ds(vir_row, BLK), pl.ds(column + i * 256, 256)] = vir
            for core in range(2):
                row = pl.multiple_of(jnp.where(my_core == core, 0, 512) + spot, 32)
                occ_ref[pl.ds(row, 32), pl.ds(column + i * 256, 256)] = occ[core * 32:(core + 1) * 32]

    lane = lax.broadcasted_iota(jnp.int32, (1, 128), 1)
    low = jnp.where(lane < BLK, 1.0, 0.0).astype(BF)
    high = jnp.where(lane < BLK, 0.0, 1.0).astype(BF)
    blank = jnp.zeros((128, 128), BF)

    def slots_of(tiles_ref, base, number, quads):
        column = number * 512
        total = None
        for quad in range(quads):
            pair = [tiles_ref[base + quad * 256 + k * 128:base + quad * 256 + (k + 1) * 128, :] for k in range(2)]
            stacked = jnp.concatenate([
                jnp.concatenate([pair[0] * low, blank], axis=1),
                jnp.concatenate([pair[0] * high, blank], axis=1),
                jnp.concatenate([blank, pair[1] * low], axis=1),
                jnp.concatenate([blank, pair[1] * high], axis=1),
            ], axis=0)
            slots = [4 * quad + t for t in range(4)]
            rows = jnp.concatenate([rows_of(meta_ref[number, TILES + slot]) for slot in slots], axis=0)
            product = jnp.dot(stacked, rows, preferred_element_type=F32)
            for t, slot in enumerate(slots):
                window = meta_ref[number, slot]
                fresh = product[t * 128:(t + 1) * 128]
                if total is None:
                    total = fresh
                else:
                    total = fresh + jnp.where(window == meta_ref[number, slot - 1], total, 0.0)
                store(total.astype(BF), window, column)

    def group(tiles_ref, base, number):
        live = meta_ref[number, 2 * TILES]

        @pl.when(live <= 8)
        def _():
            slots_of(tiles_ref, base, number, 2)

        @pl.when(live > 8)
        def _():
            slots_of(tiles_ref, base, number, 4)

    number = 0
    for tiles_ref in (own_ref, east_ref, west_ref, far_a_ref, far_b_ref):
        for base in range(0, tiles_ref.shape[0], PAY):
            group(tiles_ref, base, number)
            number += 1

    def chi(row, rows):
        return lax.dot_general(
            occ_ref[pl.ds(row, rows), :], vir_ref[...], (((1,), (1,)), ((), ())), preferred_element_type=F32
        )

    send_ref[...] = chi(512, 512).astype(BF)
    product = chi(0, 512)
    for quarter in range(4):
        keep_refs[quarter][...] = product[quarter * 128:(quarter + 1) * 128]


def chi_call(place, meta, tiles, parts):
    smem = pl.BlockSpec(memory_space=pltpu.SMEM)
    vmem = pl.BlockSpec(memory_space=pltpu.VMEM)
    return pl.pallas_call(
        chi_kernel,
        out_shape=(jax.ShapeDtypeStruct((128, RW), F32),) * 4 + (jax.ShapeDtypeStruct((512, RW), BF),),
        in_specs=[smem, smem] + [vmem] * 12,
        out_specs=(vmem,) * 5,
        scratch_shapes=[
            pltpu.VMEM((NAO, 512), BF),
            pltpu.VMEM((RW, DEPTH), BF),
            pltpu.VMEM((RW, DEPTH), BF),
        ],
        compiler_params=pltpu.CompilerParams(vmem_limit_bytes=32 * 1024 * 1024),
        cost_estimate=pl.CostEstimate(flops=12 * 10**9, bytes_accessed=8 * 2**20, transcendentals=0),
    )(place, meta, *tiles, *parts)


def together(*values):
    return lax.optimization_barrier(values)


def gather(payload, pieces):
    first = permute(pieces, scatter_target)
    own = jnp.concatenate([payload, swap_x(payload)], axis=0)
    own, first = together(own, first)
    below, above = along_z(first, 1), along_z(first, -1)
    east, west = along_y(own, 1), along_y(own, -1)
    below, above, east, west = together(below, above, east, west)
    near = swap_core(jnp.concatenate([first, above, below], axis=0))
    two_below, two_above = along_z(below[:PIECE], 1), along_z(above[:PIECE], -1)
    far_a, far_b = along_y(east[:PAY], 1), along_y(west[PAY:], -1)
    two_below, two_above, near = together(two_below, two_above, near)
    rest = swap_core(jnp.concatenate([two_above, two_below], axis=0))
    return (own, east, west, far_a, far_b), (first, above, below, two_above, two_below, near, rest)


def reduce_band(keeps, send):
    got = swap_core(send)
    parts = [got[quarter * 128:(quarter + 1) * 128] for quarter in range(4)]
    across = keeps[2] + parts[2].astype(F32)
    ahead = along_y(across[:64].astype(BF), 1)
    behind = along_y(across[64:].astype(BF), -1)
    one, three = keeps[1] + parts[1].astype(F32), keeps[3] + parts[3].astype(F32)
    up = jnp.concatenate([one[:64] + ahead.astype(F32), one[64:]], axis=0).astype(BF)
    down = jnp.concatenate([three[:64], three[64:] + behind.astype(F32)], axis=0).astype(BF)
    up, down = along_y(up, 1), along_y(down, -1)
    total = keeps[0] + parts[0].astype(F32) + up.astype(F32) + down.astype(F32)
    upper = total[:32] + swap_x(total[64:96].astype(BF)).astype(F32)
    lower = next_group(total[32:64].astype(BF), 0).astype(F32) + next_group(total[96:].astype(BF), 1).astype(F32)
    return jnp.concatenate([lower[:, :512], lower[:, 512:] + upper[:, :512], upper[:, 512:]], axis=1)


def per_device(green_occ, green_virtual, tile_values, tile_orbital, tile_window, tile_count):
    ao, pair = lax.axis_index("ao"), lax.axis_index("pair")
    x_hi, z, y, x_lo, core = device_of(ao * 16 + pair)
    place = jnp.stack([z, y, x_lo, core]).astype(jnp.int32)
    pieces = scatter_pieces(green_occ, green_virtual, z, y, core)
    payload = pack(tile_orbital, tile_window, tile_count, tile_values)
    tiles, parts = gather(payload, pieces)
    rows = [part[start + BODY:start + BODY + 1, :64] for part in tiles for start in range(0, part.shape[0], PAY)]
    meta = jnp.concatenate(rows, axis=0).astype(jnp.int32)
    *keeps, send = chi_call(place, meta, tiles, parts)
    return reduce_band(keeps, send)


def solution(mesh):
    in_specs = (
        P(None, "ao"),
        P(None, "ao"),
        P(("ao", "pair"), None, None),
        P(("ao", "pair")),
        P(("ao", "pair")),
        P(("ao", "pair")),
    )
    out_specs = P(("ao", "pair"), None)
    return jax.shard_map(
        per_device, mesh=mesh, in_specs=in_specs, out_specs=out_specs, check_vma=False
    )
```

```python
import functools

import jax
import jax.numpy as jnp
from jax import lax
from jax.experimental import pallas as pl
from jax.experimental.pallas import tpu as pltpu
from jax.sharding import PartitionSpec as P

AXES = ("ao", "pair")
BLK = 64
TILES = 16
PAIRS = TILES // 2
NAO = 2048
RW = 1024
COLS = 128
PIECE = NAO // 8
META = 16
BODY = PAIRS * 128
PAY = BODY + META
GROUPS = 8
DEPTH = GROUPS * 512
BF = jnp.bfloat16
F32 = jnp.float32


def device_of(index):
    ao, pair = index // 16, index % 16
    return ao // 8, ao % 8, pair // 4, (pair // 2) % 2, pair % 2


def index_of(x_hi, z, y, x_lo, core):
    return ((x_hi % 2) * 8 + z % 8) * 16 + ((y % 4) * 2 + x_lo % 2) * 2 + core % 2


def permute(value, where):
    pairs = [(source, index_of(*where(*device_of(source)))) for source in range(256)]
    return lax.ppermute(value, AXES, pairs)


def along_y(value, steps):
    return permute(value, lambda x_hi, z, y, x_lo, core: (x_hi, z, y + steps, x_lo, core))


def along_z(value, steps):
    return permute(value, lambda x_hi, z, y, x_lo, core: (x_hi, z + steps, y, x_lo, core))


def swap_x(value):
    return permute(value, lambda x_hi, z, y, x_lo, core: (x_hi, z, y, x_lo + 1, core))


def swap_core(value):
    return permute(value, lambda x_hi, z, y, x_lo, core: (x_hi, z, y, x_lo, core + 1))


def next_group(value, flip):
    def where(x_hi, z, y, x_lo, core):
        return (x_hi + (z == 7), z + 1, y, x_lo + flip, core)

    return permute(value, where)


Z_OFFSETS = (3, 6, 1, 5, 7, 0, 4, 2)


def scatter_target(x_hi, z, y, x_lo, core):
    target_y, target_x, target_core = z % 4, x_hi, z // 4
    target_hi = x_hi + (x_lo - target_x) % 2
    return target_hi, z + Z_OFFSETS[(y - target_y) % 4 * 2 + core], target_y, target_x, target_core


def cut_kernel(occ_ref, vir_ref, out_ref, sems):
    ao, pair = lax.axis_index("ao"), lax.axis_index("pair")
    z, y, core = lax.rem(ao, 8), pair // 4, lax.rem(pair, 2)
    case = lax.rem(y - lax.rem(z, 4) + 4, 4) * 2 + core
    target_z = z
    for number, offset in enumerate(Z_OFFSETS):
        target_z = target_z + jnp.where(case == number, offset, 0)
    copies = []
    for spot in range(2):
        start = pl.multiple_of(lax.rem(target_z + 4 * spot, 8) * PIECE, PIECE)
        for part, ref in enumerate((occ_ref, vir_ref)):
            copies.append(pltpu.make_async_copy(
                ref.at[pl.ds(start, PIECE)],
                out_ref.at[pl.ds(spot * PIECE, PIECE), pl.ds(part * COLS, COLS)],
                sems.at[spot * 2 + part],
            ))
    for copy in copies:
        copy.start()
    for copy in copies:
        copy.wait()


def cut_pieces(green_occ, green_virtual):
    return pl.pallas_call(
        cut_kernel,
        out_shape=jax.ShapeDtypeStruct((2 * PIECE, 2 * COLS), BF),
        in_specs=[pl.BlockSpec(memory_space=pl.ANY)] * 2,
        out_specs=pl.BlockSpec(memory_space=pltpu.VMEM),
        scratch_shapes=[pltpu.SemaphoreType.DMA((4,))],
    )(green_occ, green_virtual)


def pack_kernel(orbital_ref, window_ref, count_ref, tile_ref, out_ref, order_ref):
    live = count_ref[0]
    windows = [window_ref[slot] for slot in range(TILES)]
    keys = [
        jnp.where(slot < live, windows[slot], TILES) * TILES + slot for slot in range(TILES)
    ]
    ranks = [jnp.int32(0) for slot in range(TILES)]
    for first in range(TILES):
        for second in range(first + 1, TILES):
            later = (keys[second] < keys[first]).astype(jnp.int32)
            ranks[first] = ranks[first] + later
            ranks[second] = ranks[second] + (1 - later)
    for slot in range(TILES):
        order_ref[ranks[slot]] = slot
    lane = lax.broadcasted_iota(jnp.int32, (META, 128), 1)
    meta = jnp.where(lane == 32, live, jnp.zeros((META, 128), jnp.int32))
    last = jnp.int32(0)
    for slot in range(TILES):
        source = order_ref[slot]
        last = jnp.where(slot < live, window_ref[source], last)
        meta = jnp.where(lane == slot, last, meta)
        meta = jnp.where(lane == TILES + slot, orbital_ref[source], meta)
    for index in range(PAIRS):
        rows = []
        for slot in (2 * index, 2 * index + 1):
            rows.append(jnp.where(slot < live, tile_ref[order_ref[slot]].astype(F32), 0.0))
        both = jnp.concatenate(rows, axis=0)
        out_ref[pl.ds(index * 128, 128), :] = both.T.astype(BF)
    out_ref[pl.ds(BODY, META), :] = meta.astype(F32).astype(BF)


def pack(tile_orbital, tile_window, tile_count, tile_values):
    smem = pl.BlockSpec(memory_space=pltpu.SMEM)
    return pl.pallas_call(
        pack_kernel,
        out_shape=jax.ShapeDtypeStruct((PAY, 128), BF),
        in_specs=[smem, smem, smem, pl.BlockSpec(memory_space=pltpu.VMEM)],
        out_specs=pl.BlockSpec(memory_space=pltpu.VMEM),
        scratch_shapes=[pltpu.SMEM((TILES,), jnp.int32)],
    )(tile_orbital, tile_window, tile_count, tile_values)


def chi_kernel(place_ref, meta_ref, *refs):
    tile_parts, green_parts = refs[:5], refs[5:15]
    keep_refs, send_ref = refs[15:19], refs[19]
    tiles_ref, green_ref, occ_ref, vir_ref, sems = refs[20:]
    my_z, my_y, my_x, my_core = place_ref[0], place_ref[1], place_ref[2], place_ref[3]

    spots = []
    for lanes in (0, 256):
        spots += [(lanes, (0, 4)), (lanes, (1, 5)), (lanes, (7, 3)), (lanes, (2,)), (lanes, (6,))]
    copies = []
    for ref, (lanes, offsets) in zip(green_parts, spots):
        for spot, offset in enumerate(offsets):
            start = pl.multiple_of(lax.rem(my_z + offset, 8) * PIECE, PIECE)
            copies.append((
                ref.at[pl.ds(spot * PIECE, PIECE)], green_ref.at[pl.ds(start, PIECE), pl.ds(lanes, 256)]
            ))
    row = 0
    for ref in tile_parts:
        rows = ref.shape[0]
        copies.append((ref, tiles_ref.at[pl.ds(row, rows)]))
        row += rows
    copies = [pltpu.make_async_copy(source, target, sems.at[k]) for k, (source, target) in enumerate(copies)]
    for copy in copies:
        copy.start()
    occ_ref[...] = jnp.zeros_like(occ_ref)
    vir_ref[...] = jnp.zeros_like(vir_ref)
    for copy in copies:
        copy.wait()

    def rows_of(orbital):
        return green_ref[pl.ds(pl.multiple_of(orbital * BLK, BLK), BLK), :]

    def store(block, window, column):
        high, y, x = window // 8, lax.rem(window // 2, 4), lax.rem(window, 2)
        dy, dx = lax.rem(y - my_y + 4, 4), lax.rem(x - my_x + 2, 2)
        spot = ((dy * 2 + dx) * 2 + high) * 32
        vir_row = pl.multiple_of(window * BLK, BLK)
        for i in range(2):
            part = block[i * BLK:(i + 1) * BLK]
            occ = jnp.concatenate([part[:, 0:128], part[:, 256:384]], axis=1)
            vir = jnp.concatenate([part[:, 128:256], part[:, 384:512]], axis=1)
            vir_ref[pl.ds(vir_row, BLK), pl.ds(column + i * 256, 256)] = vir
            for core in range(2):
                row = pl.multiple_of(jnp.where(my_core == core, 0, 512) + spot, 32)
                occ_ref[pl.ds(row, 32), pl.ds(column + i * 256, 256)] = occ[core * 32:(core + 1) * 32]

    lane = lax.broadcasted_iota(jnp.int32, (1, 128), 1)
    low = jnp.where(lane < BLK, 1.0, 0.0).astype(BF)
    high = jnp.where(lane < BLK, 0.0, 1.0).astype(BF)
    blank = jnp.zeros((128, 128), BF)

    def slots_of(base, number, quads):
        column = number * 512
        total = None
        for quad in range(quads):
            pair = [tiles_ref[base + quad * 256 + k * 128:base + quad * 256 + (k + 1) * 128, :] for k in range(2)]
            stacked = jnp.concatenate([
                jnp.concatenate([pair[0] * low, blank], axis=1),
                jnp.concatenate([pair[0] * high, blank], axis=1),
                jnp.concatenate([blank, pair[1] * low], axis=1),
                jnp.concatenate([blank, pair[1] * high], axis=1),
            ], axis=0)
            slots = [4 * quad + t for t in range(4)]
            rows = jnp.concatenate([rows_of(meta_ref[number, TILES + slot]) for slot in slots], axis=0)
            product = jnp.dot(stacked, rows, preferred_element_type=F32)
            for t, slot in enumerate(slots):
                window = meta_ref[number, slot]
                fresh = product[t * 128:(t + 1) * 128]
                if total is None:
                    total = fresh
                else:
                    total = fresh + jnp.where(window == meta_ref[number, slot - 1], total, 0.0)
                store(total.astype(BF), window, column)

    def group(base, number):
        live = meta_ref[number, 2 * TILES]

        @pl.when(live <= 8)
        def _():
            slots_of(base, number, 2)

        @pl.when(live > 8)
        def _():
            slots_of(base, number, 4)

    for number in range(GROUPS):
        group(number * PAY, number)

    def chi(row, rows):
        return lax.dot_general(
            occ_ref[pl.ds(row, rows), :], vir_ref[...], (((1,), (1,)), ((), ())), preferred_element_type=F32
        )

    send_ref[...] = chi(512, 512).astype(BF)
    product = chi(0, 512)
    for quarter in range(4):
        keep_refs[quarter][...] = product[quarter * 128:(quarter + 1) * 128]


def chi_call(place, meta, tiles, parts):
    smem = pl.BlockSpec(memory_space=pltpu.SMEM)
    vmem = pl.BlockSpec(memory_space=pltpu.VMEM)
    return pl.pallas_call(
        chi_kernel,
        out_shape=(jax.ShapeDtypeStruct((128, RW), F32),) * 4 + (jax.ShapeDtypeStruct((512, RW), BF),),
        in_specs=[smem, smem] + [pl.BlockSpec(memory_space=pl.ANY)] * 15,
        out_specs=(vmem,) * 5,
        scratch_shapes=[
            pltpu.VMEM((GROUPS * PAY, 128), BF),
            pltpu.VMEM((NAO, 512), BF),
            pltpu.VMEM((RW, DEPTH), BF),
            pltpu.VMEM((RW, DEPTH), BF),
            pltpu.SemaphoreType.DMA((21,)),
        ],
        compiler_params=pltpu.CompilerParams(vmem_limit_bytes=32 * 1024 * 1024),
        cost_estimate=pl.CostEstimate(flops=12 * 10**9, bytes_accessed=8 * 2**20, transcendentals=0),
    )(place, meta, *tiles, *parts)


def together(*values):
    return lax.optimization_barrier(values)


def gather(payload, pieces):
    first = permute(pieces, scatter_target)
    own = jnp.concatenate([payload, swap_x(payload)], axis=0)
    own, first = together(own, first)
    single = first[:PIECE]
    green = [
        first, along_z(first, -1), along_z(first, 1), along_z(single, -2), along_z(single, 2)
    ]
    east, west = along_y(own, 1), along_y(own, -1)
    *green, east, west = together(*green, east, west)
    far_a, far_b = along_y(east[:PAY], 1), along_y(west[PAY:], -1)
    green = green + [swap_core(part) for part in green]
    return (own, east, west, far_a, far_b), green


def reduce_band(keeps, send):
    got = swap_core(send)
    parts = [got[quarter * 128:(quarter + 1) * 128] for quarter in range(4)]
    across = keeps[2] + parts[2].astype(F32)
    ahead = along_y(across[:64].astype(BF), 1)
    behind = along_y(across[64:].astype(BF), -1)
    one, three = keeps[1] + parts[1].astype(F32), keeps[3] + parts[3].astype(F32)
    up = jnp.concatenate([one[:64] + ahead.astype(F32), one[64:]], axis=0).astype(BF)
    down = jnp.concatenate([three[:64], three[64:] + behind.astype(F32)], axis=0).astype(BF)
    up, down = along_y(up, 1), along_y(down, -1)
    total = keeps[0] + parts[0].astype(F32) + up.astype(F32) + down.astype(F32)
    upper = total[:32] + swap_x(total[64:96].astype(BF)).astype(F32)
    lower = next_group(total[32:64].astype(BF), 0).astype(F32) + next_group(total[96:].astype(BF), 1).astype(F32)
    return jnp.concatenate([lower[:, :512], lower[:, 512:] + upper[:, :512], upper[:, 512:]], axis=1)


def per_device(green_occ, green_virtual, tile_values, tile_orbital, tile_window, tile_count):
    ao, pair = lax.axis_index("ao"), lax.axis_index("pair")
    x_hi, z, y, x_lo, core = device_of(ao * 16 + pair)
    place = jnp.stack([z, y, x_lo, core]).astype(jnp.int32)
    pieces = cut_pieces(green_occ, green_virtual)
    tile_values, pieces = together(tile_values, pieces)
    payload = pack(tile_orbital, tile_window, tile_count, tile_values)
    tiles, parts = gather(payload, pieces)
    rows = [part[start + BODY:start + BODY + 1, :64] for part in tiles for start in range(0, part.shape[0], PAY)]
    meta = jnp.concatenate(rows, axis=0).astype(jnp.int32)
    *keeps, send = chi_call(place, meta, tiles, parts)
    return reduce_band(keeps, send)


def solution(mesh):
    in_specs = (
        P(None, "ao"),
        P(None, "ao"),
        P(("ao", "pair"), None, None),
        P(("ao", "pair")),
        P(("ao", "pair")),
        P(("ao", "pair")),
    )
    out_specs = P(("ao", "pair"), None)
    return jax.shard_map(
        per_device, mesh=mesh, in_specs=in_specs, out_specs=out_specs, check_vma=False
    )
```

```python
import functools

import jax
import jax.numpy as jnp
from jax import lax
from jax.experimental import pallas as pl
from jax.experimental.pallas import tpu as pltpu
from jax.sharding import PartitionSpec as P

AXES = ("ao", "pair")
BLK = 64
TILES = 16
PAIRS = TILES // 2
NAO = 2048
RW = 1024
COLS = 128
PIECE = NAO // 8
META = 16
CUT = 512
BODY = PAIRS * 128
PAY = BODY + META
GROUPS = 8
DEPTH = GROUPS * 512
BF = jnp.bfloat16
F32 = jnp.float32


def device_of(index):
    ao, pair = index // 16, index % 16
    return ao // 8, ao % 8, pair // 4, (pair // 2) % 2, pair % 2


def index_of(x_hi, z, y, x_lo, core):
    return ((x_hi % 2) * 8 + z % 8) * 16 + ((y % 4) * 2 + x_lo % 2) * 2 + core % 2


def permute(value, where):
    pairs = [(source, index_of(*where(*device_of(source)))) for source in range(256)]
    return lax.ppermute(value, AXES, pairs)


def along_y(value, steps):
    return permute(value, lambda x_hi, z, y, x_lo, core: (x_hi, z, y + steps, x_lo, core))


def along_z(value, steps):
    return permute(value, lambda x_hi, z, y, x_lo, core: (x_hi, z + steps, y, x_lo, core))


def swap_x(value):
    return permute(value, lambda x_hi, z, y, x_lo, core: (x_hi, z, y, x_lo + 1, core))


def swap_core(value):
    return permute(value, lambda x_hi, z, y, x_lo, core: (x_hi, z, y, x_lo, core + 1))


def next_group(value, flip):
    def where(x_hi, z, y, x_lo, core):
        return (x_hi + (z == 7), z + 1, y, x_lo + flip, core)

    return permute(value, where)


Z_OFFSETS = (3, 6, 1, 5, 7, 0, 4, 2)


def scatter_target(x_hi, z, y, x_lo, core):
    target_y, target_x, target_core = z % 4, x_hi, z // 4
    target_hi = x_hi + (x_lo - target_x) % 2
    return target_hi, z + Z_OFFSETS[(y - target_y) % 4 * 2 + core], target_y, target_x, target_core


def piece_copies(occ_ref, vir_ref, out_ref, sems):
    ao, pair = lax.axis_index("ao"), lax.axis_index("pair")
    z, y, core = lax.rem(ao, 8), pair // 4, lax.rem(pair, 2)
    case = lax.rem(y - lax.rem(z, 4) + 4, 4) * 2 + core
    target_z = z
    for number, offset in enumerate(Z_OFFSETS):
        target_z = target_z + jnp.where(case == number, offset, 0)
    copies = []
    for spot in range(2):
        start = pl.multiple_of(lax.rem(target_z + 4 * spot, 8) * PIECE, PIECE)
        for part, ref in enumerate((occ_ref, vir_ref)):
            copies.append(pltpu.make_async_copy(
                ref.at[pl.ds(start, PIECE)],
                out_ref.at[pl.ds(spot * PIECE, PIECE), pl.ds(part * COLS, COLS)],
                sems.at[spot * 2 + part],
            ))
    return copies


def pack_kernel(
    orbital_ref, window_ref, count_ref, tile_ref, occ_ref, vir_ref, out_ref, piece_ref, order_ref, sems
):
    copies = piece_copies(occ_ref, vir_ref, piece_ref, sems)
    for copy in copies:
        copy.start()
    live = count_ref[0]
    windows = [window_ref[slot] for slot in range(TILES)]
    keys = [
        jnp.where(slot < live, windows[slot], TILES) * TILES + slot for slot in range(TILES)
    ]
    ranks = [jnp.int32(0) for slot in range(TILES)]
    for first in range(TILES):
        for second in range(first + 1, TILES):
            later = (keys[second] < keys[first]).astype(jnp.int32)
            ranks[first] = ranks[first] + later
            ranks[second] = ranks[second] + (1 - later)
    for slot in range(TILES):
        order_ref[ranks[slot]] = slot
    lane = lax.broadcasted_iota(jnp.int32, (META, 128), 1)
    meta = jnp.where(lane == 32, live, jnp.zeros((META, 128), jnp.int32))
    last = jnp.int32(0)
    for slot in range(TILES):
        source = order_ref[slot]
        last = jnp.where(slot < live, window_ref[source], last)
        meta = jnp.where(lane == slot, last, meta)
        meta = jnp.where(lane == TILES + slot, orbital_ref[source], meta)
    for index in range(PAIRS):
        rows = []
        for slot in (2 * index, 2 * index + 1):
            rows.append(jnp.where(slot < live, tile_ref[order_ref[slot]].astype(F32), 0.0))
        both = jnp.concatenate(rows, axis=0)
        out_ref[pl.ds(index * 128, 128), :] = both.T.astype(BF)
    out_ref[pl.ds(BODY, META), :] = meta.astype(F32).astype(BF)
    for copy in copies:
        copy.wait()


def pack(tile_orbital, tile_window, tile_count, tile_values, green_occ, green_virtual):
    smem = pl.BlockSpec(memory_space=pltpu.SMEM)
    vmem = pl.BlockSpec(memory_space=pltpu.VMEM)
    anywhere = pl.BlockSpec(memory_space=pl.ANY)
    return pl.pallas_call(
        pack_kernel,
        out_shape=(
            jax.ShapeDtypeStruct((PAY, 128), BF), jax.ShapeDtypeStruct((2 * PIECE, 2 * COLS), BF)
        ),
        in_specs=[smem, smem, smem, vmem, anywhere, anywhere],
        out_specs=(vmem, vmem),
        scratch_shapes=[pltpu.SMEM((TILES,), jnp.int32), pltpu.SemaphoreType.DMA((4,))],
    )(tile_orbital, tile_window, tile_count, tile_values, green_occ, green_virtual)


TILE_PARTS = tuple((number, 0, PAY, number * PAY) for number in range(6)) + (
    (4, PAY, CUT, 6 * PAY), (5, PAY, PAY - CUT, 6 * PAY + CUT),
    (6, 0, CUT, 7 * PAY), (7, 0, PAY - CUT, 7 * PAY + CUT),
)


def chi_kernel(place_ref, meta_ref, *refs):
    tile_parts, green_parts = refs[:8], refs[8:18]
    keep_refs, send_ref = refs[18:22], refs[22]
    tiles_ref, green_ref, occ_ref, vir_ref, sems = refs[23:]
    my_z, my_y, my_x, my_core = place_ref[0], place_ref[1], place_ref[2], place_ref[3]

    spots = []
    for lanes in (0, 256):
        spots += [(lanes, (0, 4)), (lanes, (1, 5)), (lanes, (7, 3)), (lanes, (2,)), (lanes, (6,))]
    copies = []
    for ref, (lanes, offsets) in zip(green_parts, spots):
        for spot, offset in enumerate(offsets):
            start = pl.multiple_of(lax.rem(my_z + offset, 8) * PIECE, PIECE)
            copies.append((
                ref.at[pl.ds(spot * PIECE, PIECE)], green_ref.at[pl.ds(start, PIECE), pl.ds(lanes, 256)]
            ))
    for part, start, rows, target in TILE_PARTS:
        copies.append((tile_parts[part].at[pl.ds(start, rows)], tiles_ref.at[pl.ds(target, rows)]))
    copies = [pltpu.make_async_copy(source, target, sems.at[k]) for k, (source, target) in enumerate(copies)]
    for copy in copies:
        copy.start()
    occ_ref[...] = jnp.zeros_like(occ_ref)
    vir_ref[...] = jnp.zeros_like(vir_ref)
    for copy in copies:
        copy.wait()

    def rows_of(orbital):
        return green_ref[pl.ds(pl.multiple_of(orbital * BLK, BLK), BLK), :]

    def store(block, window, column):
        high, y, x = window // 8, lax.rem(window // 2, 4), lax.rem(window, 2)
        dy, dx = lax.rem(y - my_y + 4, 4), lax.rem(x - my_x + 2, 2)
        spot = ((dy * 2 + dx) * 2 + high) * 32
        vir_row = pl.multiple_of(window * BLK, BLK)
        for i in range(2):
            part = block[i * BLK:(i + 1) * BLK]
            occ = jnp.concatenate([part[:, 0:128], part[:, 256:384]], axis=1)
            vir = jnp.concatenate([part[:, 128:256], part[:, 384:512]], axis=1)
            vir_ref[pl.ds(vir_row, BLK), pl.ds(column + i * 256, 256)] = vir
            for core in range(2):
                row = pl.multiple_of(jnp.where(my_core == core, 0, 512) + spot, 32)
                occ_ref[pl.ds(row, 32), pl.ds(column + i * 256, 256)] = occ[core * 32:(core + 1) * 32]

    lane = lax.broadcasted_iota(jnp.int32, (1, 128), 1)
    low = jnp.where(lane < BLK, 1.0, 0.0).astype(BF)
    high = jnp.where(lane < BLK, 0.0, 1.0).astype(BF)
    blank = jnp.zeros((128, 128), BF)

    def slots_of(base, number, quads):
        column = number * 512
        total = None
        for quad in range(quads):
            pair = [tiles_ref[base + quad * 256 + k * 128:base + quad * 256 + (k + 1) * 128, :] for k in range(2)]
            stacked = jnp.concatenate([
                jnp.concatenate([pair[0] * low, blank], axis=1),
                jnp.concatenate([pair[0] * high, blank], axis=1),
                jnp.concatenate([blank, pair[1] * low], axis=1),
                jnp.concatenate([blank, pair[1] * high], axis=1),
            ], axis=0)
            slots = [4 * quad + t for t in range(4)]
            rows = jnp.concatenate([rows_of(meta_ref[number, TILES + slot]) for slot in slots], axis=0)
            product = jnp.dot(stacked, rows, preferred_element_type=F32)
            for t, slot in enumerate(slots):
                window = meta_ref[number, slot]
                fresh = product[t * 128:(t + 1) * 128]
                if total is None:
                    total = fresh
                else:
                    total = fresh + jnp.where(window == meta_ref[number, slot - 1], total, 0.0)
                store(total.astype(BF), window, column)

    def group(base, number):
        live = meta_ref[number, 2 * TILES]

        @pl.when(live <= 8)
        def _():
            slots_of(base, number, 2)

        @pl.when(live > 8)
        def _():
            slots_of(base, number, 4)

    for number in range(GROUPS):
        group(number * PAY, number)

    def chi(row, rows):
        return lax.dot_general(
            occ_ref[pl.ds(row, rows), :], vir_ref[...], (((1,), (1,)), ((), ())), preferred_element_type=F32
        )

    send_ref[...] = chi(512, 512).astype(BF)
    product = chi(0, 512)
    for quarter in range(4):
        keep_refs[quarter][...] = product[quarter * 128:(quarter + 1) * 128]


def chi_call(place, meta, tiles, parts):
    smem = pl.BlockSpec(memory_space=pltpu.SMEM)
    vmem = pl.BlockSpec(memory_space=pltpu.VMEM)
    return pl.pallas_call(
        chi_kernel,
        out_shape=(jax.ShapeDtypeStruct((128, RW), F32),) * 4 + (jax.ShapeDtypeStruct((512, RW), BF),),
        in_specs=[smem, smem] + [pl.BlockSpec(memory_space=pl.ANY)] * 18,
        out_specs=(vmem,) * 5,
        scratch_shapes=[
            pltpu.VMEM((GROUPS * PAY, 128), BF),
            pltpu.VMEM((NAO, 512), BF),
            pltpu.VMEM((RW, DEPTH), BF),
            pltpu.VMEM((RW, DEPTH), BF),
            pltpu.SemaphoreType.DMA((26,)),
        ],
        compiler_params=pltpu.CompilerParams(vmem_limit_bytes=32 * 1024 * 1024),
        cost_estimate=pl.CostEstimate(flops=12 * 10**9, bytes_accessed=8 * 2**20, transcendentals=0),
    )(place, meta, *tiles, *parts)


def together(*values):
    return lax.optimization_barrier(values)


def gather(payload, pieces):
    first = permute(pieces, scatter_target)
    across, east, west = swap_x(payload), along_y(payload, 1), along_y(payload, -1)
    first, across = together(first, across)
    up = jnp.concatenate([across, east[:CUT]], axis=0)
    down = jnp.concatenate([across, west[CUT:]], axis=0)
    first, up, down = together(first, up, down)
    above, below = along_z(first, -1), along_z(first, 1)
    east_next, west_next = along_y(up, 1), along_y(down, -1)
    far_up, far_down = east_next[:CUT], west_next[CUT:PAY]
    near_above, near_below = above[:PIECE], below[:PIECE]
    near_above, near_below, far_up, far_down, above, below, first = together(
        near_above, near_below, far_up, far_down, above, below, first
    )
    green = [first, above, below, along_z(near_above, -1), along_z(near_below, 1)]
    far_up, far_down = along_y(far_up, 1), along_y(far_down, -1)
    green = green + [swap_core(part) for part in green]
    return (payload, across, east, west, east_next, west_next, far_up, far_down), green


def reduce_band(keeps, send):
    got = swap_core(send)
    parts = [got[quarter * 128:(quarter + 1) * 128] for quarter in range(4)]
    across = keeps[2] + parts[2].astype(F32)
    ahead = along_y(across[:64].astype(BF), 1)
    behind = along_y(across[64:].astype(BF), -1)
    one, three = keeps[1] + parts[1].astype(F32), keeps[3] + parts[3].astype(F32)
    up = jnp.concatenate([one[:64] + ahead.astype(F32), one[64:]], axis=0).astype(BF)
    down = jnp.concatenate([three[:64], three[64:] + behind.astype(F32)], axis=0).astype(BF)
    up, down = along_y(up, 1), along_y(down, -1)
    total = keeps[0] + parts[0].astype(F32) + up.astype(F32) + down.astype(F32)
    upper = total[:32] + swap_x(total[64:96].astype(BF)).astype(F32)
    lower = next_group(total[32:64].astype(BF), 0).astype(F32) + next_group(total[96:].astype(BF), 1).astype(F32)
    return jnp.concatenate([lower[:, :512], lower[:, 512:] + upper[:, :512], upper[:, 512:]], axis=1)


def per_device(green_occ, green_virtual, tile_values, tile_orbital, tile_window, tile_count):
    ao, pair = lax.axis_index("ao"), lax.axis_index("pair")
    x_hi, z, y, x_lo, core = device_of(ao * 16 + pair)
    place = jnp.stack([z, y, x_lo, core]).astype(jnp.int32)
    payload, pieces = pack(
        tile_orbital, tile_window, tile_count, tile_values, green_occ, green_virtual
    )
    tiles, parts = gather(payload, pieces)
    heads = ((0, BODY), (1, BODY), (2, BODY), (3, BODY), (4, BODY), (5, BODY), (5, PAY + BODY - CUT), (7, BODY - CUT))
    rows = [tiles[part][start:start + 1, :64] for part, start in heads]
    meta = jnp.concatenate(rows, axis=0).astype(jnp.int32)
    *keeps, send = chi_call(place, meta, tiles, parts)
    return reduce_band(keeps, send)


def solution(mesh):
    in_specs = (
        P(None, "ao"),
        P(None, "ao"),
        P(("ao", "pair"), None, None),
        P(("ao", "pair")),
        P(("ao", "pair")),
        P(("ao", "pair")),
    )
    out_specs = P(("ao", "pair"), None)
    return jax.shard_map(
        per_device, mesh=mesh, in_specs=in_specs, out_specs=out_specs, check_vma=False
    )
```

```python
import functools

import jax
import jax.numpy as jnp
from jax import lax
from jax.experimental import pallas as pl
from jax.experimental.pallas import tpu as pltpu
from jax.sharding import PartitionSpec as P

AXES = ("ao", "pair")
BLK = 64
TILES = 16
PAIRS = TILES // 2
NAO = 2048
RW = 1024
COLS = 128
PIECE = NAO // 8
META = 16
BODY = PAIRS * 128
PAY = BODY + META
GROUPS = 8
DEPTH = GROUPS * 512
BF = jnp.bfloat16
F32 = jnp.float32


def device_of(index):
    ao, pair = index // 16, index % 16
    return ao // 8, ao % 8, pair // 4, (pair // 2) % 2, pair % 2


def index_of(x_hi, z, y, x_lo, core):
    return ((x_hi % 2) * 8 + z % 8) * 16 + ((y % 4) * 2 + x_lo % 2) * 2 + core % 2


def permute(value, where):
    pairs = [(source, index_of(*where(*device_of(source)))) for source in range(256)]
    return lax.ppermute(value, AXES, pairs)


def along_y(value, steps):
    return permute(value, lambda x_hi, z, y, x_lo, core: (x_hi, z, y + steps, x_lo, core))


def along_z(value, steps):
    return permute(value, lambda x_hi, z, y, x_lo, core: (x_hi, z + steps, y, x_lo, core))


def swap_x(value):
    return permute(value, lambda x_hi, z, y, x_lo, core: (x_hi, z, y, x_lo + 1, core))


def swap_core(value):
    return permute(value, lambda x_hi, z, y, x_lo, core: (x_hi, z, y, x_lo, core + 1))


def next_group(value, flip):
    def where(x_hi, z, y, x_lo, core):
        return (x_hi + (z == 7), z + 1, y, x_lo + flip, core)

    return permute(value, where)


Z_OFFSETS = (3, 6, 1, 5, 7, 0, 4, 2)


def scatter_target(x_hi, z, y, x_lo, core):
    target_y, target_x, target_core = z % 4, x_hi, z // 4
    target_hi = x_hi + (x_lo - target_x) % 2
    return target_hi, z + Z_OFFSETS[(y - target_y) % 4 * 2 + core], target_y, target_x, target_core


def piece_copies(occ_ref, vir_ref, out_ref, sems):
    ao, pair = lax.axis_index("ao"), lax.axis_index("pair")
    z, y, core = lax.rem(ao, 8), pair // 4, lax.rem(pair, 2)
    case = lax.rem(y - lax.rem(z, 4) + 4, 4) * 2 + core
    target_z = z
    for number, offset in enumerate(Z_OFFSETS):
        target_z = target_z + jnp.where(case == number, offset, 0)
    copies = []
    for spot in range(2):
        start = pl.multiple_of(lax.rem(target_z + 4 * spot, 8) * PIECE, PIECE)
        for part, ref in enumerate((occ_ref, vir_ref)):
            copies.append(pltpu.make_async_copy(
                ref.at[pl.ds(start, PIECE)],
                out_ref.at[pl.ds(spot * PIECE, PIECE), pl.ds(part * COLS, COLS)],
                sems.at[spot * 2 + part],
            ))
    return copies


def pack_kernel(
    orbital_ref, window_ref, count_ref, tile_ref, occ_ref, vir_ref, out_ref, piece_ref, order_ref, sems
):
    copies = piece_copies(occ_ref, vir_ref, piece_ref, sems)
    for copy in copies:
        copy.start()
    live = count_ref[0]
    windows = [window_ref[slot] for slot in range(TILES)]
    keys = [
        jnp.where(slot < live, windows[slot], TILES) * TILES + slot for slot in range(TILES)
    ]
    ranks = [jnp.int32(0) for slot in range(TILES)]
    for first in range(TILES):
        for second in range(first + 1, TILES):
            later = (keys[second] < keys[first]).astype(jnp.int32)
            ranks[first] = ranks[first] + later
            ranks[second] = ranks[second] + (1 - later)
    for slot in range(TILES):
        order_ref[ranks[slot]] = slot
    lane = lax.broadcasted_iota(jnp.int32, (META, 128), 1)
    meta = jnp.where(lane == 32, live, jnp.zeros((META, 128), jnp.int32))
    last = jnp.int32(0)
    for slot in range(TILES):
        source = order_ref[slot]
        last = jnp.where(slot < live, window_ref[source], last)
        meta = jnp.where(lane == slot, last, meta)
        meta = jnp.where(lane == TILES + slot, orbital_ref[source], meta)
    for index in range(PAIRS):
        rows = []
        for slot in (2 * index, 2 * index + 1):
            rows.append(jnp.where(slot < live, tile_ref[order_ref[slot]].astype(F32), 0.0))
        both = jnp.concatenate(rows, axis=0)
        out_ref[pl.ds(index * 128, 128), :] = both.T.astype(BF)
    out_ref[pl.ds(BODY, META), :] = meta.astype(F32).astype(BF)
    for copy in copies:
        copy.wait()


def pack(tile_orbital, tile_window, tile_count, tile_values, green_occ, green_virtual):
    smem = pl.BlockSpec(memory_space=pltpu.SMEM)
    vmem = pl.BlockSpec(memory_space=pltpu.VMEM)
    anywhere = pl.BlockSpec(memory_space=pl.ANY)
    return pl.pallas_call(
        pack_kernel,
        out_shape=(
            jax.ShapeDtypeStruct((PAY, 128), BF), jax.ShapeDtypeStruct((2 * PIECE, 2 * COLS), BF)
        ),
        in_specs=[smem, smem, smem, vmem, anywhere, anywhere],
        out_specs=(vmem, vmem),
        scratch_shapes=[pltpu.SMEM((TILES,), jnp.int32), pltpu.SemaphoreType.DMA((4,))],
    )(tile_orbital, tile_window, tile_count, tile_values, green_occ, green_virtual)


PART_OFFSETS = ((0, 4), (1, 5), (7, 3), (6, 2))


def chi_kernel(place_ref, meta_ref, *refs):
    tile_parts, green_parts = refs[:8], refs[8:16]
    keep_refs, send_ref = refs[16:20], refs[20]
    tiles_ref, green_ref, occ_ref, vir_ref, sems = refs[21:]
    my_z, my_y, my_x, my_core = place_ref[0], place_ref[1], place_ref[2], place_ref[3]

    copies = []
    for number, ref in enumerate(green_parts):
        for spot, offset in enumerate(PART_OFFSETS[number % 4]):
            start = pl.multiple_of(lax.rem(my_z + offset, 8) * PIECE, PIECE)
            lanes = number // 4 * 256
            copies.append((
                ref.at[pl.ds(spot * PIECE, PIECE)], green_ref.at[pl.ds(start, PIECE), pl.ds(lanes, 256)]
            ))
    for number, ref in enumerate(tile_parts):
        copies.append((ref, tiles_ref.at[pl.ds(number * PAY, PAY)]))
    copies = [pltpu.make_async_copy(source, target, sems.at[k]) for k, (source, target) in enumerate(copies)]
    for copy in copies:
        copy.start()
    occ_ref[...] = jnp.zeros_like(occ_ref)
    vir_ref[...] = jnp.zeros_like(vir_ref)
    for copy in copies:
        copy.wait()

    def rows_of(orbital):
        return green_ref[pl.ds(pl.multiple_of(orbital * BLK, BLK), BLK), :]

    def store(block, window, column):
        high, y, x = window // 8, lax.rem(window // 2, 4), lax.rem(window, 2)
        dy, dx = lax.rem(y - my_y + 4, 4), lax.rem(x - my_x + 2, 2)
        spot = ((dy * 2 + dx) * 2 + high) * 32
        vir_row = pl.multiple_of(window * BLK, BLK)
        for i in range(2):
            part = block[i * BLK:(i + 1) * BLK]
            occ = jnp.concatenate([part[:, 0:128], part[:, 256:384]], axis=1)
            vir = jnp.concatenate([part[:, 128:256], part[:, 384:512]], axis=1)
            vir_ref[pl.ds(vir_row, BLK), pl.ds(column + i * 256, 256)] = vir
            for core in range(2):
                row = pl.multiple_of(jnp.where(my_core == core, 0, 512) + spot, 32)
                occ_ref[pl.ds(row, 32), pl.ds(column + i * 256, 256)] = occ[core * 32:(core + 1) * 32]

    lane = lax.broadcasted_iota(jnp.int32, (1, 128), 1)
    low = jnp.where(lane < BLK, 1.0, 0.0).astype(BF)
    high = jnp.where(lane < BLK, 0.0, 1.0).astype(BF)
    blank = jnp.zeros((128, 128), BF)

    def slots_of(base, number, quads):
        column = pl.multiple_of(number * 512, 512)
        total = None
        for quad in range(quads):
            pair = [
                tiles_ref[pl.ds(pl.multiple_of(base + quad * 256 + k * 128, 16), 128), :] for k in range(2)
            ]
            stacked = jnp.concatenate([
                jnp.concatenate([pair[0] * low, blank], axis=1),
                jnp.concatenate([pair[0] * high, blank], axis=1),
                jnp.concatenate([blank, pair[1] * low], axis=1),
                jnp.concatenate([blank, pair[1] * high], axis=1),
            ], axis=0)
            slots = [4 * quad + t for t in range(4)]
            rows = jnp.concatenate([rows_of(meta_ref[number, TILES + slot]) for slot in slots], axis=0)
            product = jnp.dot(stacked, rows, preferred_element_type=F32)
            for t, slot in enumerate(slots):
                window = meta_ref[number, slot]
                fresh = product[t * 128:(t + 1) * 128]
                if total is None:
                    total = fresh
                else:
                    total = fresh + jnp.where(window == meta_ref[number, slot - 1], total, 0.0)
                store(total.astype(BF), window, column)

    @pl.loop(0, GROUPS)
    def _(number):
        base = number * PAY
        live = meta_ref[number, 2 * TILES]

        @pl.when(live <= 8)
        def _():
            slots_of(base, number, 2)

        @pl.when(live > 8)
        def _():
            slots_of(base, number, 4)

    def chi(row, rows):
        return lax.dot_general(
            occ_ref[pl.ds(row, rows), :], vir_ref[...], (((1,), (1,)), ((), ())), preferred_element_type=F32
        )

    send_ref[...] = chi(512, 512).astype(BF)
    product = chi(0, 512)
    for quarter in range(4):
        keep_refs[quarter][...] = product[quarter * 128:(quarter + 1) * 128]


def chi_call(place, meta, tiles, parts):
    smem = pl.BlockSpec(memory_space=pltpu.SMEM)
    vmem = pl.BlockSpec(memory_space=pltpu.VMEM)
    return pl.pallas_call(
        chi_kernel,
        out_shape=(jax.ShapeDtypeStruct((128, RW), F32),) * 4 + (jax.ShapeDtypeStruct((512, RW), BF),),
        in_specs=[smem, smem] + [pl.BlockSpec(memory_space=pl.ANY)] * 16,
        out_specs=(vmem,) * 5,
        scratch_shapes=[
            pltpu.VMEM((GROUPS * PAY, 128), BF),
            pltpu.VMEM((NAO, 512), BF),
            pltpu.VMEM((RW, DEPTH), BF),
            pltpu.VMEM((RW, DEPTH), BF),
            pltpu.SemaphoreType.DMA((24,)),
        ],
        compiler_params=pltpu.CompilerParams(vmem_limit_bytes=32 * 1024 * 1024),
        cost_estimate=pl.CostEstimate(flops=12 * 10**9, bytes_accessed=8 * 2**20, transcendentals=0),
    )(place, meta, *tiles, *parts)


def gather_tiles(payload):
    across = swap_x(payload)
    east, west = along_y(payload, 1), along_y(payload, -1)
    east_across, west_across = along_y(across, 1), along_y(across, -1)
    return payload, across, east, west, east_across, west_across, along_y(east, 1), along_y(west_across, -1)


def gather_green(pieces):
    first = permute(pieces, scatter_target)
    above, below = along_z(first, -1), along_z(first, 1)
    parts = (first, above, below, along_z(below, 1))
    return parts + tuple(swap_core(part) for part in parts)


def reduce_band(keeps, send):
    got = swap_core(send)
    parts = [got[quarter * 128:(quarter + 1) * 128] for quarter in range(4)]
    across = keeps[2] + parts[2].astype(F32)
    ahead = along_y(across[:64].astype(BF), 1)
    behind = along_y(across[64:].astype(BF), -1)
    one, three = keeps[1] + parts[1].astype(F32), keeps[3] + parts[3].astype(F32)
    up = jnp.concatenate([one[:64] + ahead.astype(F32), one[64:]], axis=0).astype(BF)
    down = jnp.concatenate([three[:64], three[64:] + behind.astype(F32)], axis=0).astype(BF)
    up, down = along_y(up, 1), along_y(down, -1)
    total = keeps[0] + parts[0].astype(F32) + up.astype(F32) + down.astype(F32)
    upper = total[:32] + swap_x(total[64:96].astype(BF)).astype(F32)
    lower = next_group(total[32:64].astype(BF), 0).astype(F32) + next_group(total[96:].astype(BF), 1).astype(F32)
    return jnp.concatenate([lower[:, :512], lower[:, 512:] + upper[:, :512], upper[:, 512:]], axis=1)


def per_device(green_occ, green_virtual, tile_values, tile_orbital, tile_window, tile_count):
    ao, pair = lax.axis_index("ao"), lax.axis_index("pair")
    x_hi, z, y, x_lo, core = device_of(ao * 16 + pair)
    place = jnp.stack([z, y, x_lo, core]).astype(jnp.int32)
    payload, pieces = pack(
        tile_orbital, tile_window, tile_count, tile_values, green_occ, green_virtual
    )
    tiles, parts = gather_tiles(payload), gather_green(pieces)
    rows = [part[BODY:BODY + 1, :64] for part in tiles]
    meta = jnp.concatenate(rows, axis=0).astype(jnp.int32)
    *keeps, send = chi_call(place, meta, tiles, parts)
    return reduce_band(keeps, send)


def solution(mesh):
    in_specs = (
        P(None, "ao"),
        P(None, "ao"),
        P(("ao", "pair"), None, None),
        P(("ao", "pair")),
        P(("ao", "pair")),
        P(("ao", "pair")),
    )
    out_specs = P(("ao", "pair"), None)
    return jax.shard_map(
        per_device, mesh=mesh, in_specs=in_specs, out_specs=out_specs, check_vma=False
    )
```

```python
import functools

import jax
import jax.numpy as jnp
from jax import lax
from jax.experimental import pallas as pl
from jax.experimental.pallas import tpu as pltpu
from jax.sharding import PartitionSpec as P

AXES = ("ao", "pair")
BLK = 64
TILES = 16
PAIRS = TILES // 2
NAO = 2048
RW = 1024
COLS = 128
PIECE = NAO // 8
META = 16
BODY = PAIRS * 128
PAY = BODY + META
GROUPS = 8
DEPTH = GROUPS * 512
BF = jnp.bfloat16
F32 = jnp.float32


def device_of(index):
    ao, pair = index // 16, index % 16
    return ao // 8, ao % 8, pair // 4, (pair // 2) % 2, pair % 2


def index_of(x_hi, z, y, x_lo, core):
    return ((x_hi % 2) * 8 + z % 8) * 16 + ((y % 4) * 2 + x_lo % 2) * 2 + core % 2


def permute(value, where):
    pairs = [(source, index_of(*where(*device_of(source)))) for source in range(256)]
    return lax.ppermute(value, AXES, pairs)


def along_y(value, steps):
    return permute(value, lambda x_hi, z, y, x_lo, core: (x_hi, z, y + steps, x_lo, core))


def along_z(value, steps):
    return permute(value, lambda x_hi, z, y, x_lo, core: (x_hi, z + steps, y, x_lo, core))


def swap_x(value):
    return permute(value, lambda x_hi, z, y, x_lo, core: (x_hi, z, y, x_lo + 1, core))


def swap_core(value):
    return permute(value, lambda x_hi, z, y, x_lo, core: (x_hi, z, y, x_lo, core + 1))


def next_group(value, flip):
    def where(x_hi, z, y, x_lo, core):
        return (x_hi + (z == 7), z + 1, y, x_lo + flip, core)

    return permute(value, where)


Z_OFFSETS = (3, 6, 1, 5, 7, 0, 4, 2)


def scatter_target(x_hi, z, y, x_lo, core):
    target_y, target_x, target_core = z % 4, x_hi, z // 4
    target_hi = x_hi + (x_lo - target_x) % 2
    return target_hi, z + Z_OFFSETS[(y - target_y) % 4 * 2 + core], target_y, target_x, target_core


def piece_copies(occ_ref, vir_ref, out_ref, sems):
    ao, pair = lax.axis_index("ao"), lax.axis_index("pair")
    z, y, core = lax.rem(ao, 8), pair // 4, lax.rem(pair, 2)
    case = lax.rem(y - lax.rem(z, 4) + 4, 4) * 2 + core
    target_z = z
    for number, offset in enumerate(Z_OFFSETS):
        target_z = target_z + jnp.where(case == number, offset, 0)
    copies = []
    for spot in range(2):
        start = pl.multiple_of(lax.rem(target_z + 4 * spot, 8) * PIECE, PIECE)
        for part, ref in enumerate((occ_ref, vir_ref)):
            copies.append(pltpu.make_async_copy(
                ref.at[pl.ds(start, PIECE)],
                out_ref.at[pl.ds(spot * PIECE, PIECE), pl.ds(part * COLS, COLS)],
                sems.at[spot * 2 + part],
            ))
    return copies


def cut_kernel(occ_ref, vir_ref, piece_ref, sems):
    copies = piece_copies(occ_ref, vir_ref, piece_ref, sems)
    for copy in copies:
        copy.start()
    for copy in copies:
        copy.wait()


def cut_pieces(green_occ, green_virtual):
    return pl.pallas_call(
        cut_kernel,
        out_shape=jax.ShapeDtypeStruct((2 * PIECE, 2 * COLS), BF),
        in_specs=[pl.BlockSpec(memory_space=pl.ANY)] * 2,
        out_specs=pl.BlockSpec(memory_space=pltpu.VMEM),
        scratch_shapes=[pltpu.SemaphoreType.DMA((4,))],
    )(green_occ, green_virtual)


def pack_kernel(orbital_ref, window_ref, count_ref, tile_ref, unused_ref, out_ref, order_ref):
    live = count_ref[0]
    windows = [window_ref[slot] for slot in range(TILES)]
    keys = [
        jnp.where(slot < live, windows[slot], TILES) * TILES + slot for slot in range(TILES)
    ]
    ranks = [jnp.int32(0) for slot in range(TILES)]
    for first in range(TILES):
        for second in range(first + 1, TILES):
            later = (keys[second] < keys[first]).astype(jnp.int32)
            ranks[first] = ranks[first] + later
            ranks[second] = ranks[second] + (1 - later)
    for slot in range(TILES):
        order_ref[ranks[slot]] = slot
    lane = lax.broadcasted_iota(jnp.int32, (META, 128), 1)
    meta = jnp.where(lane == 32, live, jnp.zeros((META, 128), jnp.int32))
    last = jnp.int32(0)
    for slot in range(TILES):
        source = order_ref[slot]
        last = jnp.where(slot < live, window_ref[source], last)
        meta = jnp.where(lane == slot, last, meta)
        meta = jnp.where(lane == TILES + slot, orbital_ref[source], meta)
    for index in range(PAIRS):
        rows = []
        for slot in (2 * index, 2 * index + 1):
            rows.append(jnp.where(slot < live, tile_ref[order_ref[slot]].astype(F32), 0.0))
        both = jnp.concatenate(rows, axis=0)
        out_ref[pl.ds(index * 128, 128), :] = both.T.astype(BF)
    out_ref[pl.ds(BODY, META), :] = meta.astype(F32).astype(BF)


def pack(tile_orbital, tile_window, tile_count, tile_values, pieces):
    smem = pl.BlockSpec(memory_space=pltpu.SMEM)
    vmem = pl.BlockSpec(memory_space=pltpu.VMEM)
    return pl.pallas_call(
        pack_kernel,
        out_shape=jax.ShapeDtypeStruct((PAY, 128), BF),
        in_specs=[smem, smem, smem, vmem, pl.BlockSpec(memory_space=pl.ANY)],
        out_specs=vmem,
        scratch_shapes=[pltpu.SMEM((TILES,), jnp.int32)],
    )(tile_orbital, tile_window, tile_count, tile_values, pieces)


PART_OFFSETS = ((0, 4), (1, 5), (7, 3), (6, 2))


def chi_kernel(*refs):
    tile_parts, green_parts = refs[:8], refs[8:16]
    keep_refs, send_ref = refs[16:20], refs[20]
    tiles_ref, green_ref, occ_ref, vir_ref, flat_ref, meta_ref, sems = refs[21:]
    ao, pair = lax.axis_index("ao"), lax.axis_index("pair")
    my_z, my_y, my_x, my_core = lax.rem(ao, 8), pair // 4, lax.rem(pair // 2, 2), lax.rem(pair, 2)

    copies = []
    for number, ref in enumerate(green_parts):
        for spot, offset in enumerate(PART_OFFSETS[number % 4]):
            start = pl.multiple_of(lax.rem(my_z + offset, 8) * PIECE, PIECE)
            lanes = number // 4 * 256
            copies.append((
                ref.at[pl.ds(spot * PIECE, PIECE)], green_ref.at[pl.ds(start, PIECE), pl.ds(lanes, 256)]
            ))
    for number, ref in enumerate(tile_parts):
        copies.append((ref, tiles_ref.at[pl.ds(number * PAY, PAY)]))
    copies = [pltpu.make_async_copy(source, target, sems.at[k]) for k, (source, target) in enumerate(copies)]
    for copy in copies:
        copy.start()
    occ_ref[...] = jnp.zeros_like(occ_ref)
    for copy in copies[16:]:
        copy.wait()
    for number in range(GROUPS):
        head = tiles_ref[pl.ds(number * PAY + BODY, META), :].astype(F32).astype(jnp.int32)
        flat_ref[pl.ds(number, 1), :] = head[:1]
    to_scalars = pltpu.make_async_copy(flat_ref, meta_ref, sems.at[24])
    to_scalars.start()
    vir_ref[...] = jnp.zeros_like(vir_ref)
    for copy in copies[:16]:
        copy.wait()
    to_scalars.wait()

    def rows_of(orbital):
        return green_ref[pl.ds(pl.multiple_of(orbital * BLK, BLK), BLK), :]

    def store(block, window, column):
        high, y, x = window // 8, lax.rem(window // 2, 4), lax.rem(window, 2)
        dy, dx = lax.rem(y - my_y + 4, 4), lax.rem(x - my_x + 2, 2)
        spot = ((dy * 2 + dx) * 2 + high) * 32
        vir_row = pl.multiple_of(window * BLK, BLK)
        for i in range(2):
            part = block[i * BLK:(i + 1) * BLK]
            occ = jnp.concatenate([part[:, 0:128], part[:, 256:384]], axis=1)
            vir = jnp.concatenate([part[:, 128:256], part[:, 384:512]], axis=1)
            vir_ref[pl.ds(vir_row, BLK), pl.ds(column + i * 256, 256)] = vir
            for core in range(2):
                row = pl.multiple_of(jnp.where(my_core == core, 0, 512) + spot, 32)
                occ_ref[pl.ds(row, 32), pl.ds(column + i * 256, 256)] = occ[core * 32:(core + 1) * 32]

    lane = lax.broadcasted_iota(jnp.int32, (1, 128), 1)
    low = jnp.where(lane < BLK, 1.0, 0.0).astype(BF)
    high = jnp.where(lane < BLK, 0.0, 1.0).astype(BF)
    blank = jnp.zeros((128, 128), BF)

    def slots_of(base, number, quads):
        column = pl.multiple_of(number * 512, 512)
        total = None
        for quad in range(quads):
            pair = [
                tiles_ref[pl.ds(pl.multiple_of(base + quad * 256 + k * 128, 16), 128), :] for k in range(2)
            ]
            stacked = jnp.concatenate([
                jnp.concatenate([pair[0] * low, blank], axis=1),
                jnp.concatenate([pair[0] * high, blank], axis=1),
                jnp.concatenate([blank, pair[1] * low], axis=1),
                jnp.concatenate([blank, pair[1] * high], axis=1),
            ], axis=0)
            slots = [4 * quad + t for t in range(4)]
            rows = jnp.concatenate([rows_of(meta_ref[number, TILES + slot]) for slot in slots], axis=0)
            product = jnp.dot(stacked, rows, preferred_element_type=F32)
            for t, slot in enumerate(slots):
                window = meta_ref[number, slot]
                fresh = product[t * 128:(t + 1) * 128]
                if total is None:
                    total = fresh
                else:
                    total = fresh + jnp.where(window == meta_ref[number, slot - 1], total, 0.0)
                store(total.astype(BF), window, column)

    @pl.loop(0, GROUPS)
    def _(number):
        base = number * PAY
        live = meta_ref[number, 2 * TILES]

        @pl.when(live <= 8)
        def _():
            slots_of(base, number, 2)

        @pl.when(live > 8)
        def _():
            slots_of(base, number, 4)

    def chi(row, rows):
        return lax.dot_general(
            occ_ref[pl.ds(row, rows), :], vir_ref[...], (((1,), (1,)), ((), ())), preferred_element_type=F32
        )

    send_ref[...] = chi(512, 512).astype(BF)
    product = chi(0, 512)
    for quarter in range(4):
        keep_refs[quarter][...] = product[quarter * 128:(quarter + 1) * 128]


def chi_call(tiles, parts):
    vmem = pl.BlockSpec(memory_space=pltpu.VMEM)
    return pl.pallas_call(
        chi_kernel,
        out_shape=(jax.ShapeDtypeStruct((128, RW), F32),) * 4 + (jax.ShapeDtypeStruct((512, RW), BF),),
        in_specs=[pl.BlockSpec(memory_space=pl.ANY)] * 16,
        out_specs=(vmem,) * 5,
        scratch_shapes=[
            pltpu.VMEM((GROUPS * PAY, 128), BF),
            pltpu.VMEM((NAO, 512), BF),
            pltpu.VMEM((RW, DEPTH), BF),
            pltpu.VMEM((RW, DEPTH), BF),
            pltpu.VMEM((GROUPS, 128), jnp.int32),
            pltpu.SMEM((GROUPS, 128), jnp.int32),
            pltpu.SemaphoreType.DMA((25,)),
        ],
        compiler_params=pltpu.CompilerParams(vmem_limit_bytes=32 * 1024 * 1024),
        cost_estimate=pl.CostEstimate(flops=12 * 10**9, bytes_accessed=8 * 2**20, transcendentals=0),
    )(*tiles, *parts)


def gather_tiles(payload):
    across = swap_x(payload)
    east, west = along_y(payload, 1), along_y(payload, -1)
    east_across, west_across = along_y(across, 1), along_y(across, -1)
    return payload, across, east, west, east_across, west_across, along_y(east, 1), along_y(west_across, -1)


def gather_green(pieces):
    first = permute(pieces, scatter_target)
    above, below = along_z(first, -1), along_z(first, 1)
    parts = (first, above, below, along_z(below, 1))
    return parts + tuple(swap_core(part) for part in parts)


def reduce_band(keeps, send):
    got = swap_core(send)
    parts = [got[quarter * 128:(quarter + 1) * 128] for quarter in range(4)]
    across = keeps[2] + parts[2].astype(F32)
    ahead = along_y(across[:64].astype(BF), 1)
    behind = along_y(across[64:].astype(BF), -1)
    one, three = keeps[1] + parts[1].astype(F32), keeps[3] + parts[3].astype(F32)
    up = jnp.concatenate([one[:64] + ahead.astype(F32), one[64:]], axis=0).astype(BF)
    down = jnp.concatenate([three[:64], three[64:] + behind.astype(F32)], axis=0).astype(BF)
    up, down = along_y(up, 1), along_y(down, -1)
    total = keeps[0] + parts[0].astype(F32) + up.astype(F32) + down.astype(F32)
    upper = total[:32] + swap_x(total[64:96].astype(BF)).astype(F32)
    lower = next_group(total[32:64].astype(BF), 0).astype(F32) + next_group(total[96:].astype(BF), 1).astype(F32)
    return jnp.concatenate([lower[:, :512], lower[:, 512:] + upper[:, :512], upper[:, 512:]], axis=1)


def per_device(green_occ, green_virtual, tile_values, tile_orbital, tile_window, tile_count):
    pieces = cut_pieces(green_occ, green_virtual)
    payload = pack(tile_orbital, tile_window, tile_count, tile_values, pieces)
    tiles, parts = gather_tiles(payload), gather_green(pieces)
    *keeps, send = chi_call(tiles, parts)
    return reduce_band(keeps, send)


def solution(mesh):
    in_specs = (
        P(None, "ao"),
        P(None, "ao"),
        P(("ao", "pair"), None, None),
        P(("ao", "pair")),
        P(("ao", "pair")),
        P(("ao", "pair")),
    )
    out_specs = P(("ao", "pair"), None)
    return jax.shard_map(
        per_device, mesh=mesh, in_specs=in_specs, out_specs=out_specs, check_vma=False
    )
```

```python
import functools

import jax
import jax.numpy as jnp
from jax import lax
from jax.experimental import pallas as pl
from jax.experimental.pallas import tpu as pltpu
from jax.sharding import PartitionSpec as P

AXES = ("ao", "pair")
BLK = 64
TILES = 16
PAIRS = TILES // 2
NAO = 2048
RW = 1024
COLS = 128
PIECE = NAO // 8
META = 16
BODY = PAIRS * 128
PAY = BODY + META
GROUPS = 8
DEPTH = GROUPS * 512
BF = jnp.bfloat16
F32 = jnp.float32


def device_of(index):
    ao, pair = index // 16, index % 16
    return ao // 8, ao % 8, pair // 4, (pair // 2) % 2, pair % 2


def index_of(x_hi, z, y, x_lo, core):
    return ((x_hi % 2) * 8 + z % 8) * 16 + ((y % 4) * 2 + x_lo % 2) * 2 + core % 2


def permute(value, where):
    pairs = [(source, index_of(*where(*device_of(source)))) for source in range(256)]
    return lax.ppermute(value, AXES, pairs)


def along_y(value, steps):
    return permute(value, lambda x_hi, z, y, x_lo, core: (x_hi, z, y + steps, x_lo, core))


def along_z(value, steps):
    return permute(value, lambda x_hi, z, y, x_lo, core: (x_hi, z + steps, y, x_lo, core))


def swap_x(value):
    return permute(value, lambda x_hi, z, y, x_lo, core: (x_hi, z, y, x_lo + 1, core))


def swap_core(value):
    return permute(value, lambda x_hi, z, y, x_lo, core: (x_hi, z, y, x_lo, core + 1))


def next_group(value, flip):
    def where(x_hi, z, y, x_lo, core):
        return (x_hi + (z == 7), z + 1, y, x_lo + flip, core)

    return permute(value, where)


Z_OFFSETS = (3, 6, 1, 5, 7, 0, 4, 2)


def scatter_target(x_hi, z, y, x_lo, core):
    target_y, target_x, target_core = z % 4, x_hi, z // 4
    target_hi = x_hi + (x_lo - target_x) % 2
    return target_hi, z + Z_OFFSETS[(y - target_y) % 4 * 2 + core], target_y, target_x, target_core


def piece_copies(occ_ref, vir_ref, out_ref, sems):
    ao, pair = lax.axis_index("ao"), lax.axis_index("pair")
    z, y, core = lax.rem(ao, 8), pair // 4, lax.rem(pair, 2)
    case = lax.rem(y - lax.rem(z, 4) + 4, 4) * 2 + core
    target_z = z
    for number, offset in enumerate(Z_OFFSETS):
        target_z = target_z + jnp.where(case == number, offset, 0)
    copies = []
    for spot in range(2):
        start = pl.multiple_of(lax.rem(target_z + 4 * spot, 8) * PIECE, PIECE)
        for part, ref in enumerate((occ_ref, vir_ref)):
            copies.append(pltpu.make_async_copy(
                ref.at[pl.ds(start, PIECE)],
                out_ref.at[pl.ds(spot * PIECE, PIECE), pl.ds(part * COLS, COLS)],
                sems.at[spot * 2 + part],
            ))
    return copies


def cut_kernel(occ_ref, vir_ref, piece_ref, sems):
    copies = piece_copies(occ_ref, vir_ref, piece_ref, sems)
    for copy in copies:
        copy.start()
    for copy in copies:
        copy.wait()


def cut_pieces(green_occ, green_virtual):
    return pl.pallas_call(
        cut_kernel,
        out_shape=jax.ShapeDtypeStruct((2 * PIECE, 2 * COLS), BF),
        in_specs=[pl.BlockSpec(memory_space=pl.ANY)] * 2,
        out_specs=pl.BlockSpec(memory_space=pltpu.VMEM),
        scratch_shapes=[pltpu.SemaphoreType.DMA((4,))],
    )(green_occ, green_virtual)


def pack_kernel(orbital_ref, window_ref, count_ref, tile_ref, unused_ref, out_ref, order_ref):
    live = count_ref[0]
    windows = [window_ref[slot] for slot in range(TILES)]
    keys = [
        jnp.where(slot < live, windows[slot], TILES) * TILES + slot for slot in range(TILES)
    ]
    ranks = [jnp.int32(0) for slot in range(TILES)]
    for first in range(TILES):
        for second in range(first + 1, TILES):
            later = (keys[second] < keys[first]).astype(jnp.int32)
            ranks[first] = ranks[first] + later
            ranks[second] = ranks[second] + (1 - later)
    for slot in range(TILES):
        order_ref[ranks[slot]] = slot
    lane = lax.broadcasted_iota(jnp.int32, (META, 128), 1)
    meta = jnp.where(lane == 32, live, jnp.zeros((META, 128), jnp.int32))
    last = jnp.int32(0)
    for slot in range(TILES):
        source = order_ref[slot]
        last = jnp.where(slot < live, window_ref[source], last)
        meta = jnp.where(lane == slot, last, meta)
        meta = jnp.where(lane == TILES + slot, orbital_ref[source], meta)
    for index in range(PAIRS):
        rows = []
        for slot in (2 * index, 2 * index + 1):
            rows.append(jnp.where(slot < live, tile_ref[order_ref[slot]].astype(F32), 0.0))
        both = jnp.concatenate(rows, axis=0)
        out_ref[pl.ds(index * 128, 128), :] = both.T.astype(BF)
    out_ref[pl.ds(BODY, META), :] = meta.astype(F32).astype(BF)


def pack(tile_orbital, tile_window, tile_count, tile_values, pieces):
    smem = pl.BlockSpec(memory_space=pltpu.SMEM)
    vmem = pl.BlockSpec(memory_space=pltpu.VMEM)
    return pl.pallas_call(
        pack_kernel,
        out_shape=pltpu.VMEM((PAY, 128), BF),
        in_specs=[smem, smem, smem, vmem, pl.BlockSpec(memory_space=pl.ANY)],
        out_specs=vmem,
        scratch_shapes=[pltpu.SMEM((TILES,), jnp.int32)],
    )(tile_orbital, tile_window, tile_count, tile_values, pieces)


PART_OFFSETS = ((0, 4), (1, 5), (7, 3), (6, 2))


def chi_kernel(*refs):
    tile_parts, green_parts = refs[:8], refs[8:16]
    send_ref, occ_ref, vir_ref = refs[16:19]
    tiles_ref, green_ref, flat_ref, meta_ref, sems = refs[19:]
    ao, pair = lax.axis_index("ao"), lax.axis_index("pair")
    my_z, my_y, my_x, my_core = lax.rem(ao, 8), pair // 4, lax.rem(pair // 2, 2), lax.rem(pair, 2)

    copies = []
    for number, ref in enumerate(green_parts):
        for spot, offset in enumerate(PART_OFFSETS[number % 4]):
            start = pl.multiple_of(lax.rem(my_z + offset, 8) * PIECE, PIECE)
            lanes = number // 4 * 256
            copies.append((
                ref.at[pl.ds(spot * PIECE, PIECE)], green_ref.at[pl.ds(start, PIECE), pl.ds(lanes, 256)]
            ))
    for number, ref in enumerate(tile_parts):
        copies.append((ref, tiles_ref.at[pl.ds(number * PAY, PAY)]))
    copies = [pltpu.make_async_copy(source, target, sems.at[k]) for k, (source, target) in enumerate(copies)]
    for copy in copies:
        copy.start()
    occ_ref[...] = jnp.zeros_like(occ_ref)
    for copy in copies[16:]:
        copy.wait()
    for number in range(GROUPS):
        head = tiles_ref[pl.ds(number * PAY + BODY, META), :].astype(F32).astype(jnp.int32)
        flat_ref[pl.ds(number, 1), :] = head[:1]
    to_scalars = pltpu.make_async_copy(flat_ref, meta_ref, sems.at[24])
    to_scalars.start()
    vir_ref[...] = jnp.zeros_like(vir_ref)
    for copy in copies[:16]:
        copy.wait()
    to_scalars.wait()

    def rows_of(orbital):
        return green_ref[pl.ds(pl.multiple_of(orbital * BLK, BLK), BLK), :]

    def store(block, window, column):
        high, y, x = window // 8, lax.rem(window // 2, 4), lax.rem(window, 2)
        dy, dx = lax.rem(y - my_y + 4, 4), lax.rem(x - my_x + 2, 2)
        spot = ((dy * 2 + dx) * 2 + high) * 32
        vir_row = pl.multiple_of(window * BLK, BLK)
        for i in range(2):
            part = block[i * BLK:(i + 1) * BLK]
            occ = jnp.concatenate([part[:, 0:128], part[:, 256:384]], axis=1)
            vir = jnp.concatenate([part[:, 128:256], part[:, 384:512]], axis=1)
            vir_ref[pl.ds(vir_row, BLK), pl.ds(column + i * 256, 256)] = vir
            for core in range(2):
                row = pl.multiple_of(jnp.where(my_core == core, 0, 512) + spot, 32)
                occ_ref[pl.ds(row, 32), pl.ds(column + i * 256, 256)] = occ[core * 32:(core + 1) * 32]

    lane = lax.broadcasted_iota(jnp.int32, (1, 128), 1)
    low = jnp.where(lane < BLK, 1.0, 0.0).astype(BF)
    high = jnp.where(lane < BLK, 0.0, 1.0).astype(BF)
    blank = jnp.zeros((128, 128), BF)

    def slots_of(base, number, quads):
        column = pl.multiple_of(number * 512, 512)
        total = None
        for quad in range(quads):
            pair = [
                tiles_ref[pl.ds(pl.multiple_of(base + quad * 256 + k * 128, 16), 128), :] for k in range(2)
            ]
            stacked = jnp.concatenate([
                jnp.concatenate([pair[0] * low, blank], axis=1),
                jnp.concatenate([pair[0] * high, blank], axis=1),
                jnp.concatenate([blank, pair[1] * low], axis=1),
                jnp.concatenate([blank, pair[1] * high], axis=1),
            ], axis=0)
            slots = [4 * quad + t for t in range(4)]
            rows = jnp.concatenate([rows_of(meta_ref[number, TILES + slot]) for slot in slots], axis=0)
            product = jnp.dot(stacked, rows, preferred_element_type=F32)
            for t, slot in enumerate(slots):
                window = meta_ref[number, slot]
                fresh = product[t * 128:(t + 1) * 128]
                if total is None:
                    total = fresh
                else:
                    total = fresh + jnp.where(window == meta_ref[number, slot - 1], total, 0.0)
                store(total.astype(BF), window, column)

    @pl.loop(0, GROUPS)
    def _(number):
        base = number * PAY
        live = meta_ref[number, 2 * TILES]

        @pl.when(live <= 8)
        def _():
            slots_of(base, number, 2)

        @pl.when(live > 8)
        def _():
            slots_of(base, number, 4)

    send_ref[...] = chi_rows(occ_ref, vir_ref, 512).astype(BF)


def chi_rows(occ_ref, vir_ref, row):
    return lax.dot_general(
        occ_ref[pl.ds(row, 512), :], vir_ref[...], (((1,), (1,)), ((), ())), preferred_element_type=F32
    )


def keep_kernel(occ_ref, vir_ref, *keep_refs):
    product = chi_rows(occ_ref, vir_ref, 0)
    for quarter in range(4):
        keep_refs[quarter][...] = product[quarter * 128:(quarter + 1) * 128]


def chi_call(tiles, parts):
    vmem = pl.BlockSpec(memory_space=pltpu.VMEM)
    send, occ, vir = pl.pallas_call(
        chi_kernel,
        out_shape=(
            jax.ShapeDtypeStruct((512, RW), BF), pltpu.VMEM((RW, DEPTH), BF), pltpu.VMEM((RW, DEPTH), BF)
        ),
        in_specs=[pl.BlockSpec(memory_space=pl.ANY)] * 16,
        out_specs=(vmem,) * 3,
        scratch_shapes=[
            pltpu.VMEM((GROUPS * PAY, 128), BF),
            pltpu.VMEM((NAO, 512), BF),
            pltpu.VMEM((GROUPS, 128), jnp.int32),
            pltpu.SMEM((GROUPS, 128), jnp.int32),
            pltpu.SemaphoreType.DMA((25,)),
        ],
        compiler_params=pltpu.CompilerParams(vmem_limit_bytes=20 * 1024 * 1024),
        cost_estimate=pl.CostEstimate(flops=8 * 10**9, bytes_accessed=8 * 2**20, transcendentals=0),
    )(*tiles, *parts)
    keeps = pl.pallas_call(
        keep_kernel,
        out_shape=(jax.ShapeDtypeStruct((128, RW), F32),) * 4,
        in_specs=[vmem, vmem],
        out_specs=(vmem,) * 4,
        compiler_params=pltpu.CompilerParams(vmem_limit_bytes=12 * 1024 * 1024),
        cost_estimate=pl.CostEstimate(flops=4 * 10**9, bytes_accessed=4 * 2**20, transcendentals=0),
    )(occ, vir)
    return keeps, send


def gather_tiles(payload):
    across = swap_x(payload)
    east, west = along_y(payload, 1), along_y(payload, -1)
    east_across, west_across = along_y(across, 1), along_y(across, -1)
    return payload, across, east, west, east_across, west_across, along_y(east, 1), along_y(west_across, -1)


def gather_green(pieces):
    first = permute(pieces, scatter_target)
    above, below = along_z(first, -1), along_z(first, 1)
    parts = (first, above, below, along_z(below, 1))
    return parts + tuple(swap_core(part) for part in parts)


def reduce_band(keeps, send):
    got = swap_core(send)
    parts = [got[quarter * 128:(quarter + 1) * 128] for quarter in range(4)]
    across = keeps[2] + parts[2].astype(F32)
    ahead = along_y(across[:64].astype(BF), 1)
    behind = along_y(across[64:].astype(BF), -1)
    one, three = keeps[1] + parts[1].astype(F32), keeps[3] + parts[3].astype(F32)
    up = jnp.concatenate([one[:64] + ahead.astype(F32), one[64:]], axis=0).astype(BF)
    down = jnp.concatenate([three[:64], three[64:] + behind.astype(F32)], axis=0).astype(BF)
    up, down = along_y(up, 1), along_y(down, -1)
    total = keeps[0] + parts[0].astype(F32) + up.astype(F32) + down.astype(F32)
    upper = total[:32] + swap_x(total[64:96].astype(BF)).astype(F32)
    lower = next_group(total[32:64].astype(BF), 0).astype(F32) + next_group(total[96:].astype(BF), 1).astype(F32)
    return jnp.concatenate([lower[:, :512], lower[:, 512:] + upper[:, :512], upper[:, 512:]], axis=1)


def per_device(green_occ, green_virtual, tile_values, tile_orbital, tile_window, tile_count):
    pieces = cut_pieces(green_occ, green_virtual)
    payload = pack(tile_orbital, tile_window, tile_count, tile_values, pieces)
    tiles, parts = gather_tiles(payload), gather_green(pieces)
    keeps, send = chi_call(tiles, parts)
    return reduce_band(keeps, send)


def solution(mesh):
    in_specs = (
        P(None, "ao"),
        P(None, "ao"),
        P(("ao", "pair"), None, None),
        P(("ao", "pair")),
        P(("ao", "pair")),
        P(("ao", "pair")),
    )
    out_specs = P(("ao", "pair"), None)
    return jax.shard_map(
        per_device, mesh=mesh, in_specs=in_specs, out_specs=out_specs, check_vma=False
    )
```

```python
import functools

import jax
import jax.numpy as jnp
from jax import lax
from jax.experimental import pallas as pl
from jax.experimental.pallas import tpu as pltpu
from jax.sharding import PartitionSpec as P

AXES = ("ao", "pair")
BLK = 64
TILES = 16
PAIRS = TILES // 2
NAO = 2048
RW = 1024
COLS = 128
PIECE = NAO // 8
META = 16
BODY = PAIRS * 128
PAY = BODY + META
GROUPS = 8
DEPTH = GROUPS * 512
BF = jnp.bfloat16
F32 = jnp.float32


def device_of(index):
    ao, pair = index // 16, index % 16
    return ao // 8, ao % 8, pair // 4, (pair // 2) % 2, pair % 2


def index_of(x_hi, z, y, x_lo, core):
    return ((x_hi % 2) * 8 + z % 8) * 16 + ((y % 4) * 2 + x_lo % 2) * 2 + core % 2


def permute(value, where):
    pairs = [(source, index_of(*where(*device_of(source)))) for source in range(256)]
    return lax.ppermute(value, AXES, pairs)


def along_y(value, steps):
    return permute(value, lambda x_hi, z, y, x_lo, core: (x_hi, z, y + steps, x_lo, core))


def along_z(value, steps):
    return permute(value, lambda x_hi, z, y, x_lo, core: (x_hi, z + steps, y, x_lo, core))


def swap_x(value):
    return permute(value, lambda x_hi, z, y, x_lo, core: (x_hi, z, y, x_lo + 1, core))


def swap_core(value):
    return permute(value, lambda x_hi, z, y, x_lo, core: (x_hi, z, y, x_lo, core + 1))


def next_group(value, flip):
    def where(x_hi, z, y, x_lo, core):
        return (x_hi + (z == 7), z + 1, y, x_lo + flip, core)

    return permute(value, where)


Z_OFFSETS = (3, 6, 1, 5, 7, 0, 4, 2)


def scatter_target(x_hi, z, y, x_lo, core):
    target_y, target_x, target_core = z % 4, x_hi, z // 4
    target_hi = x_hi + (x_lo - target_x) % 2
    return target_hi, z + Z_OFFSETS[(y - target_y) % 4 * 2 + core], target_y, target_x, target_core


def piece_copies(occ_ref, vir_ref, out_ref, sems):
    ao, pair = lax.axis_index("ao"), lax.axis_index("pair")
    z, y, core = lax.rem(ao, 8), pair // 4, lax.rem(pair, 2)
    case = lax.rem(y - lax.rem(z, 4) + 4, 4) * 2 + core
    target_z = z
    for number, offset in enumerate(Z_OFFSETS):
        target_z = target_z + jnp.where(case == number, offset, 0)
    copies = []
    for spot in range(2):
        start = pl.multiple_of(lax.rem(target_z + 4 * spot, 8) * PIECE, PIECE)
        for part, ref in enumerate((occ_ref, vir_ref)):
            copies.append(pltpu.make_async_copy(
                ref.at[pl.ds(start, PIECE)],
                out_ref.at[pl.ds(spot * PIECE, PIECE), pl.ds(part * COLS, COLS)],
                sems.at[spot * 2 + part],
            ))
    return copies


def cut_kernel(occ_ref, vir_ref, piece_ref, sems):
    copies = piece_copies(occ_ref, vir_ref, piece_ref, sems)
    for copy in copies:
        copy.start()
    for copy in copies:
        copy.wait()


def cut_pieces(green_occ, green_virtual):
    return pl.pallas_call(
        cut_kernel,
        out_shape=jax.ShapeDtypeStruct((2 * PIECE, 2 * COLS), BF),
        in_specs=[pl.BlockSpec(memory_space=pl.ANY)] * 2,
        out_specs=pl.BlockSpec(memory_space=pltpu.VMEM),
        scratch_shapes=[pltpu.SemaphoreType.DMA((4,))],
    )(green_occ, green_virtual)


def pack_kernel(orbital_ref, window_ref, count_ref, tile_ref, unused_ref, out_ref, order_ref):
    live = count_ref[0]
    windows = [window_ref[slot] for slot in range(TILES)]
    keys = [
        jnp.where(slot < live, windows[slot], TILES) * TILES + slot for slot in range(TILES)
    ]
    ranks = [jnp.int32(0) for slot in range(TILES)]
    for first in range(TILES):
        for second in range(first + 1, TILES):
            later = (keys[second] < keys[first]).astype(jnp.int32)
            ranks[first] = ranks[first] + later
            ranks[second] = ranks[second] + (1 - later)
    for slot in range(TILES):
        order_ref[ranks[slot]] = slot
    lane = lax.broadcasted_iota(jnp.int32, (META, 128), 1)
    meta = jnp.where(lane == 32, live, jnp.zeros((META, 128), jnp.int32))
    last = jnp.int32(0)
    for slot in range(TILES):
        source = order_ref[slot]
        last = jnp.where(slot < live, window_ref[source], last)
        meta = jnp.where(lane == slot, last, meta)
        meta = jnp.where(lane == TILES + slot, orbital_ref[source], meta)
    for index in range(PAIRS):
        rows = []
        for slot in (2 * index, 2 * index + 1):
            rows.append(jnp.where(slot < live, tile_ref[order_ref[slot]].astype(F32), 0.0))
        both = jnp.concatenate(rows, axis=0)
        out_ref[pl.ds(index * 128, 128), :] = both.T.astype(BF)
    out_ref[pl.ds(BODY, META), :] = meta.astype(F32).astype(BF)


def pack(tile_orbital, tile_window, tile_count, tile_values, pieces):
    smem = pl.BlockSpec(memory_space=pltpu.SMEM)
    vmem = pl.BlockSpec(memory_space=pltpu.VMEM)
    return pl.pallas_call(
        pack_kernel,
        out_shape=pltpu.VMEM((PAY, 128), BF),
        in_specs=[smem, smem, smem, vmem, pl.BlockSpec(memory_space=pl.ANY)],
        out_specs=vmem,
        scratch_shapes=[pltpu.SMEM((TILES,), jnp.int32)],
    )(tile_orbital, tile_window, tile_count, tile_values, pieces)


SEND_ROW, KEEP_ROW = 256, 640
PART_OFFSETS = ((0, 4), (1, 5), (7, 3), (6, 2))


def chi_kernel(*refs):
    tile_parts, green_parts = refs[:8], refs[8:16]
    keep_ref, send_ref, occ_ref, vir_ref = refs[16:20]
    tiles_ref, green_ref, flat_ref, meta_ref, sems = refs[20:]
    ao, pair = lax.axis_index("ao"), lax.axis_index("pair")
    my_z, my_y, my_x, my_core = lax.rem(ao, 8), pair // 4, lax.rem(pair // 2, 2), lax.rem(pair, 2)

    copies = []
    for number, ref in enumerate(green_parts):
        for spot, offset in enumerate(PART_OFFSETS[number % 4]):
            start = pl.multiple_of(lax.rem(my_z + offset, 8) * PIECE, PIECE)
            lanes = number // 4 * 256
            copies.append((
                ref.at[pl.ds(spot * PIECE, PIECE)], green_ref.at[pl.ds(start, PIECE), pl.ds(lanes, 256)]
            ))
    for number, ref in enumerate(tile_parts):
        copies.append((ref, tiles_ref.at[pl.ds(number * PAY, PAY)]))
    copies = [pltpu.make_async_copy(source, target, sems.at[k]) for k, (source, target) in enumerate(copies)]
    for copy in copies:
        copy.start()
    occ_ref[...] = jnp.zeros_like(occ_ref)
    for copy in copies[16:]:
        copy.wait()
    for number in range(GROUPS):
        head = tiles_ref[pl.ds(number * PAY + BODY, META), :].astype(F32).astype(jnp.int32)
        flat_ref[pl.ds(number, 1), :] = head[:1]
    to_scalars = pltpu.make_async_copy(flat_ref, meta_ref, sems.at[24])
    to_scalars.start()
    vir_ref[...] = jnp.zeros_like(vir_ref)
    for copy in copies[:16]:
        copy.wait()
    to_scalars.wait()

    def rows_of(orbital):
        return green_ref[pl.ds(pl.multiple_of(orbital * BLK, BLK), BLK), :]

    def store(block, window, column):
        high, y, x = window // 8, lax.rem(window // 2, 4), lax.rem(window, 2)
        dy, dx = lax.rem(y - my_y + 4, 4), lax.rem(x - my_x + 2, 2)
        spot = (dx * 2 + high) * 32
        far = dy == 2
        rest = jnp.where(dy == 3, 256, dy * 128)
        vir_row = pl.multiple_of(window * BLK, BLK)
        for i in range(2):
            part = block[i * BLK:(i + 1) * BLK]
            occ = jnp.concatenate([part[:, 0:128], part[:, 256:384]], axis=1)
            vir = jnp.concatenate([part[:, 128:256], part[:, 384:512]], axis=1)
            vir_ref[pl.ds(vir_row, BLK), pl.ds(column + i * 256, 256)] = vir
            for core in range(2):
                row = jnp.where(
                    my_core == core, jnp.where(far, 0, KEEP_ROW + rest), jnp.where(far, 128, SEND_ROW + rest)
                )
                row = pl.multiple_of(row + spot, 32)
                occ_ref[pl.ds(row, 32), pl.ds(column + i * 256, 256)] = occ[core * 32:(core + 1) * 32]

    lane = lax.broadcasted_iota(jnp.int32, (1, 128), 1)
    low = jnp.where(lane < BLK, 1.0, 0.0).astype(BF)
    high = jnp.where(lane < BLK, 0.0, 1.0).astype(BF)
    blank = jnp.zeros((128, 128), BF)

    def slots_of(base, number, quads):
        column = pl.multiple_of(number * 512, 512)
        total = None
        for quad in range(quads):
            pair = [
                tiles_ref[pl.ds(pl.multiple_of(base + quad * 256 + k * 128, 16), 128), :] for k in range(2)
            ]
            stacked = jnp.concatenate([
                jnp.concatenate([pair[0] * low, blank], axis=1),
                jnp.concatenate([pair[0] * high, blank], axis=1),
                jnp.concatenate([blank, pair[1] * low], axis=1),
                jnp.concatenate([blank, pair[1] * high], axis=1),
            ], axis=0)
            slots = [4 * quad + t for t in range(4)]
            rows = jnp.concatenate([rows_of(meta_ref[number, TILES + slot]) for slot in slots], axis=0)
            product = jnp.dot(stacked, rows, preferred_element_type=F32)
            for t, slot in enumerate(slots):
                window = meta_ref[number, slot]
                fresh = product[t * 128:(t + 1) * 128]
                if total is None:
                    total = fresh
                else:
                    total = fresh + jnp.where(window == meta_ref[number, slot - 1], total, 0.0)
                store(total.astype(BF), window, column)

    @pl.loop(0, GROUPS)
    def _(number):
        base = number * PAY
        live = meta_ref[number, 2 * TILES]

        @pl.when(live <= 8)
        def _():
            slots_of(base, number, 2)

        @pl.when(live > 8)
        def _():
            slots_of(base, number, 4)

    product = chi_rows(occ_ref, vir_ref, 0, SEND_ROW)
    keep_ref[...] = product[:128]
    send_ref[...] = product[128:].astype(BF)


def chi_rows(occ_ref, vir_ref, row, rows):
    return lax.dot_general(
        occ_ref[pl.ds(row, rows), :], vir_ref[...], (((1,), (1,)), ((), ())), preferred_element_type=F32
    )


def send_kernel(occ_ref, vir_ref, send_ref):
    send_ref[...] = chi_rows(occ_ref, vir_ref, SEND_ROW, KEEP_ROW - SEND_ROW).astype(BF)


def first_kernel(keep_ref, got_ref, unused_ref, ahead_ref, behind_ref):
    total = keep_ref[...] + got_ref[...].astype(F32)
    ahead_ref[...] = total[:64].astype(BF)
    behind_ref[...] = total[64:].astype(BF)


def keep_kernel(occ_ref, vir_ref, unused_ref, *keep_refs):
    product = chi_rows(occ_ref, vir_ref, KEEP_ROW, RW - KEEP_ROW)
    for number, keep_ref in enumerate(keep_refs):
        keep_ref[...] = product[number * 128:(number + 1) * 128]


def chi_call(tiles, parts):
    vmem = pl.BlockSpec(memory_space=pltpu.VMEM)
    limits = pltpu.CompilerParams(vmem_limit_bytes=12 * 1024 * 1024)
    cost = pl.CostEstimate(flops=4 * 10**9, bytes_accessed=4 * 2**20, transcendentals=0)
    keep, send, occ, vir = pl.pallas_call(
        chi_kernel,
        out_shape=(
            jax.ShapeDtypeStruct((128, RW), F32), jax.ShapeDtypeStruct((128, RW), BF),
            pltpu.VMEM((RW, DEPTH), BF), pltpu.VMEM((RW, DEPTH), BF),
        ),
        in_specs=[pl.BlockSpec(memory_space=pl.ANY)] * 16,
        out_specs=(vmem,) * 4,
        scratch_shapes=[
            pltpu.VMEM((GROUPS * PAY, 128), BF),
            pltpu.VMEM((NAO, 512), BF),
            pltpu.VMEM((GROUPS, 128), jnp.int32),
            pltpu.SMEM((GROUPS, 128), jnp.int32),
            pltpu.SemaphoreType.DMA((25,)),
        ],
        compiler_params=pltpu.CompilerParams(vmem_limit_bytes=20 * 1024 * 1024),
        cost_estimate=pl.CostEstimate(flops=8 * 10**9, bytes_accessed=8 * 2**20, transcendentals=0),
    )(*tiles, *parts)
    got = swap_core(send)
    send_rest = pl.pallas_call(
        send_kernel,
        out_shape=jax.ShapeDtypeStruct((KEEP_ROW - SEND_ROW, RW), BF),
        in_specs=[vmem] * 2,
        out_specs=vmem,
        compiler_params=limits,
        cost_estimate=cost,
    )(occ, vir)
    ahead, behind = pl.pallas_call(
        first_kernel,
        out_shape=(jax.ShapeDtypeStruct((64, RW), BF),) * 2,
        in_specs=[vmem, vmem, pl.BlockSpec(memory_space=pl.ANY)],
        out_specs=(vmem,) * 2,
        compiler_params=limits,
    )(keep, got, send_rest)
    send_rest, ahead = lax.optimization_barrier((send_rest, ahead))
    keeps = pl.pallas_call(
        keep_kernel,
        out_shape=(jax.ShapeDtypeStruct((128, RW), F32),) * 3,
        in_specs=[vmem, vmem, pl.BlockSpec(memory_space=pl.ANY)],
        out_specs=(vmem,) * 3,
        compiler_params=limits,
        cost_estimate=cost,
    )(occ, vir, ahead)
    return along_y(ahead, 1), along_y(behind, -1), swap_core(send_rest), keeps


def gather_tiles(payload):
    across = swap_x(payload)
    east, west = along_y(payload, 1), along_y(payload, -1)
    east_across, west_across = along_y(across, 1), along_y(across, -1)
    return payload, across, east, west, east_across, west_across, along_y(east, 1), along_y(west_across, -1)


def gather_green(pieces):
    first = permute(pieces, scatter_target)
    above, below = along_z(first, -1), along_z(first, 1)
    parts = (first, above, below, along_z(below, 1))
    return parts + tuple(swap_core(part) for part in parts)


def reduce_band(ahead, behind, got, keeps):
    own, one, three = [
        keep + got[number * 128:(number + 1) * 128].astype(F32) for number, keep in enumerate(keeps)
    ]
    up = jnp.concatenate([one[:64] + ahead.astype(F32), one[64:]], axis=0).astype(BF)
    down = jnp.concatenate([three[:64], three[64:] + behind.astype(F32)], axis=0).astype(BF)
    up, down = along_y(up, 1), along_y(down, -1)
    total = own + up.astype(F32) + down.astype(F32)
    upper = total[:32] + swap_x(total[64:96].astype(BF)).astype(F32)
    lower = next_group(total[32:64].astype(BF), 0).astype(F32) + next_group(total[96:].astype(BF), 1).astype(F32)
    return jnp.concatenate([lower[:, :512], lower[:, 512:] + upper[:, :512], upper[:, 512:]], axis=1)


def per_device(green_occ, green_virtual, tile_values, tile_orbital, tile_window, tile_count):
    pieces = cut_pieces(green_occ, green_virtual)
    payload = pack(tile_orbital, tile_window, tile_count, tile_values, pieces)
    tiles, parts = gather_tiles(payload), gather_green(pieces)
    return reduce_band(*chi_call(tiles, parts))


def solution(mesh):
    in_specs = (
        P(None, "ao"),
        P(None, "ao"),
        P(("ao", "pair"), None, None),
        P(("ao", "pair")),
        P(("ao", "pair")),
        P(("ao", "pair")),
    )
    out_specs = P(("ao", "pair"), None)
    return jax.shard_map(
        per_device, mesh=mesh, in_specs=in_specs, out_specs=out_specs, check_vma=False
    )
```

```python
import functools

import jax
import jax.numpy as jnp
from jax import lax
from jax.experimental import pallas as pl
from jax.experimental.pallas import tpu as pltpu
from jax.sharding import PartitionSpec as P

AXES = ("ao", "pair")
BLK = 64
TILES = 16
PAIRS = TILES // 2
NAO = 2048
RW = 1024
COLS = 128
PIECE = NAO // 8
META = 16
BODY = PAIRS * 128
PAY = BODY + META
GROUPS = 8
DEPTH = GROUPS * 512
BF = jnp.bfloat16
F32 = jnp.float32


def device_of(index):
    ao, pair = index // 16, index % 16
    return ao // 8, ao % 8, pair // 4, (pair // 2) % 2, pair % 2


def index_of(x_hi, z, y, x_lo, core):
    return ((x_hi % 2) * 8 + z % 8) * 16 + ((y % 4) * 2 + x_lo % 2) * 2 + core % 2


def permute(value, where):
    pairs = [(source, index_of(*where(*device_of(source)))) for source in range(256)]
    return lax.ppermute(value, AXES, pairs)


def along_y(value, steps):
    return permute(value, lambda x_hi, z, y, x_lo, core: (x_hi, z, y + steps, x_lo, core))


def along_z(value, steps):
    return permute(value, lambda x_hi, z, y, x_lo, core: (x_hi, z + steps, y, x_lo, core))


def swap_x(value):
    return permute(value, lambda x_hi, z, y, x_lo, core: (x_hi, z, y, x_lo + 1, core))


def swap_core(value):
    return permute(value, lambda x_hi, z, y, x_lo, core: (x_hi, z, y, x_lo, core + 1))


def next_group(value, flip):
    def where(x_hi, z, y, x_lo, core):
        return (x_hi + (z == 7), z + 1, y, x_lo + flip, core)

    return permute(value, where)


Z_OFFSETS = (3, 6, 1, 5, 7, 0, 4, 2)


def scatter_target(x_hi, z, y, x_lo, core):
    target_y, target_x, target_core = z % 4, x_hi, z // 4
    target_hi = x_hi + (x_lo - target_x) % 2
    return target_hi, z + Z_OFFSETS[(y - target_y) % 4 * 2 + core], target_y, target_x, target_core


def piece_copies(occ_ref, vir_ref, out_ref, sems):
    ao, pair = lax.axis_index("ao"), lax.axis_index("pair")
    z, y, core = lax.rem(ao, 8), pair // 4, lax.rem(pair, 2)
    case = lax.rem(y - lax.rem(z, 4) + 4, 4) * 2 + core
    target_z = z
    for number, offset in enumerate(Z_OFFSETS):
        target_z = target_z + jnp.where(case == number, offset, 0)
    copies = []
    for spot in range(2):
        start = pl.multiple_of(lax.rem(target_z + 4 * spot, 8) * PIECE, PIECE)
        for part, ref in enumerate((occ_ref, vir_ref)):
            copies.append(pltpu.make_async_copy(
                ref.at[pl.ds(start, PIECE)],
                out_ref.at[pl.ds(spot * PIECE, PIECE), pl.ds(part * COLS, COLS)],
                sems.at[spot * 2 + part],
            ))
    return copies


def cut_kernel(occ_ref, vir_ref, piece_ref, sems):
    copies = piece_copies(occ_ref, vir_ref, piece_ref, sems)
    for copy in copies:
        copy.start()
    for copy in copies:
        copy.wait()


def cut_pieces(green_occ, green_virtual):
    return pl.pallas_call(
        cut_kernel,
        out_shape=jax.ShapeDtypeStruct((2 * PIECE, 2 * COLS), BF),
        in_specs=[pl.BlockSpec(memory_space=pl.ANY)] * 2,
        out_specs=pl.BlockSpec(memory_space=pltpu.VMEM),
        scratch_shapes=[pltpu.SemaphoreType.DMA((4,))],
    )(green_occ, green_virtual)


def pack_kernel(orbital_ref, window_ref, count_ref, tile_ref, unused_ref, out_ref, order_ref):
    live = count_ref[0]
    windows = [window_ref[slot] for slot in range(TILES)]
    keys = [
        jnp.where(slot < live, windows[slot], TILES) * TILES + slot for slot in range(TILES)
    ]
    ranks = [jnp.int32(0) for slot in range(TILES)]
    for first in range(TILES):
        for second in range(first + 1, TILES):
            later = (keys[second] < keys[first]).astype(jnp.int32)
            ranks[first] = ranks[first] + later
            ranks[second] = ranks[second] + (1 - later)
    for slot in range(TILES):
        order_ref[ranks[slot]] = slot
    lane = lax.broadcasted_iota(jnp.int32, (META, 128), 1)
    meta = jnp.where(lane == 32, live, jnp.zeros((META, 128), jnp.int32))
    last = jnp.int32(0)
    for slot in range(TILES):
        source = order_ref[slot]
        last = jnp.where(slot < live, window_ref[source], last)
        meta = jnp.where(lane == slot, last, meta)
        meta = jnp.where(lane == TILES + slot, orbital_ref[source], meta)
    for index in range(PAIRS):
        rows = []
        for slot in (2 * index, 2 * index + 1):
            rows.append(jnp.where(slot < live, tile_ref[order_ref[slot]].astype(F32), 0.0))
        both = jnp.concatenate(rows, axis=0)
        out_ref[pl.ds(index * 128, 128), :] = both.T.astype(BF)
    out_ref[pl.ds(BODY, META), :] = meta.astype(F32).astype(BF)


def pack(tile_orbital, tile_window, tile_count, tile_values, pieces):
    smem = pl.BlockSpec(memory_space=pltpu.SMEM)
    vmem = pl.BlockSpec(memory_space=pltpu.VMEM)
    return pl.pallas_call(
        pack_kernel,
        out_shape=pltpu.VMEM((PAY, 128), BF),
        in_specs=[smem, smem, smem, vmem, pl.BlockSpec(memory_space=pl.ANY)],
        out_specs=vmem,
        scratch_shapes=[pltpu.SMEM((TILES,), jnp.int32)],
    )(tile_orbital, tile_window, tile_count, tile_values, pieces)


SEND_ROW, KEEP_ROW = 256, 640
PART_OFFSETS = ((0, 4), (1, 5), (7, 3), (6, 2))


def chi_kernel(*refs):
    tile_parts, green_parts = refs[:8], refs[8:16]
    keep_ref, send_ref, occ_ref, vir_ref = refs[16:20]
    tiles_ref, green_ref, flat_ref, meta_ref, sems = refs[20:]
    ao, pair = lax.axis_index("ao"), lax.axis_index("pair")
    my_z, my_y, my_x, my_core = lax.rem(ao, 8), pair // 4, lax.rem(pair // 2, 2), lax.rem(pair, 2)

    for number, ref in enumerate(tile_parts):
        tiles_ref[pl.ds(number * PAY, PAY), :] = ref[...]
        head = ref[pl.ds(BODY, META), :].astype(F32).astype(jnp.int32)
        flat_ref[pl.ds(number, 1), :] = head[:1]
    to_scalars = pltpu.make_async_copy(flat_ref, meta_ref, sems.at[0])
    to_scalars.start()
    for number, ref in enumerate(green_parts):
        for spot, offset in enumerate(PART_OFFSETS[number % 4]):
            start = pl.multiple_of(lax.rem(my_z + offset, 8) * PIECE, PIECE)
            lanes = number // 4 * 256
            green_ref[pl.ds(start, PIECE), lanes:lanes + 256] = ref[spot * PIECE:(spot + 1) * PIECE, :]
    occ_ref[...] = jnp.zeros_like(occ_ref)
    vir_ref[...] = jnp.zeros_like(vir_ref)
    to_scalars.wait()

    def rows_of(orbital):
        return green_ref[pl.ds(pl.multiple_of(orbital * BLK, BLK), BLK), :]

    def store(block, window, column):
        high, y, x = window // 8, lax.rem(window // 2, 4), lax.rem(window, 2)
        dy, dx = lax.rem(y - my_y + 4, 4), lax.rem(x - my_x + 2, 2)
        spot = (dx * 2 + high) * 32
        far = dy == 2
        rest = jnp.where(dy == 3, 256, dy * 128)
        vir_row = pl.multiple_of(window * BLK, BLK)
        for i in range(2):
            part = block[i * BLK:(i + 1) * BLK]
            occ = jnp.concatenate([part[:, 0:128], part[:, 256:384]], axis=1)
            vir = jnp.concatenate([part[:, 128:256], part[:, 384:512]], axis=1)
            vir_ref[pl.ds(vir_row, BLK), pl.ds(column + i * 256, 256)] = vir
            for core in range(2):
                row = jnp.where(
                    my_core == core, jnp.where(far, 0, KEEP_ROW + rest), jnp.where(far, 128, SEND_ROW + rest)
                )
                row = pl.multiple_of(row + spot, 32)
                occ_ref[pl.ds(row, 32), pl.ds(column + i * 256, 256)] = occ[core * 32:(core + 1) * 32]

    lane = lax.broadcasted_iota(jnp.int32, (1, 128), 1)
    low = jnp.where(lane < BLK, 1.0, 0.0).astype(BF)
    high = jnp.where(lane < BLK, 0.0, 1.0).astype(BF)
    blank = jnp.zeros((128, 128), BF)

    def slots_of(base, number, quads):
        column = pl.multiple_of(number * 512, 512)
        total = None
        for quad in range(quads):
            pair = [
                tiles_ref[pl.ds(pl.multiple_of(base + quad * 256 + k * 128, 16), 128), :] for k in range(2)
            ]
            stacked = jnp.concatenate([
                jnp.concatenate([pair[0] * low, blank], axis=1),
                jnp.concatenate([pair[0] * high, blank], axis=1),
                jnp.concatenate([blank, pair[1] * low], axis=1),
                jnp.concatenate([blank, pair[1] * high], axis=1),
            ], axis=0)
            slots = [4 * quad + t for t in range(4)]
            rows = jnp.concatenate([rows_of(meta_ref[number, TILES + slot]) for slot in slots], axis=0)
            product = jnp.dot(stacked, rows, preferred_element_type=F32)
            for t, slot in enumerate(slots):
                window = meta_ref[number, slot]
                fresh = product[t * 128:(t + 1) * 128]
                if total is None:
                    total = fresh
                else:
                    total = fresh + jnp.where(window == meta_ref[number, slot - 1], total, 0.0)
                store(total.astype(BF), window, column)

    @pl.loop(0, GROUPS)
    def _(number):
        base = number * PAY
        live = meta_ref[number, 2 * TILES]

        @pl.when(live <= 8)
        def _():
            slots_of(base, number, 2)

        @pl.when(live > 8)
        def _():
            slots_of(base, number, 4)

    product = chi_rows(occ_ref, vir_ref, 0, SEND_ROW)
    keep_ref[...] = product[:128]
    send_ref[...] = product[128:].astype(BF)


def chi_rows(occ_ref, vir_ref, row, rows):
    return lax.dot_general(
        occ_ref[pl.ds(row, rows), :], vir_ref[...], (((1,), (1,)), ((), ())), preferred_element_type=F32
    )


def send_kernel(occ_ref, vir_ref, send_ref):
    send_ref[...] = chi_rows(occ_ref, vir_ref, SEND_ROW, KEEP_ROW - SEND_ROW).astype(BF)


def first_kernel(keep_ref, got_ref, unused_ref, ahead_ref, behind_ref):
    total = keep_ref[...] + got_ref[...].astype(F32)
    ahead_ref[...] = total[:64].astype(BF)
    behind_ref[...] = total[64:].astype(BF)


def keep_kernel(occ_ref, vir_ref, unused_ref, *keep_refs):
    product = chi_rows(occ_ref, vir_ref, KEEP_ROW, RW - KEEP_ROW)
    for number, keep_ref in enumerate(keep_refs):
        keep_ref[...] = product[number * 128:(number + 1) * 128]


def chi_call(tiles, parts):
    vmem = pl.BlockSpec(memory_space=pltpu.VMEM)
    limits = pltpu.CompilerParams(vmem_limit_bytes=12 * 1024 * 1024)
    cost = pl.CostEstimate(flops=4 * 10**9, bytes_accessed=4 * 2**20, transcendentals=0)
    keep, send, occ, vir = pl.pallas_call(
        chi_kernel,
        out_shape=(
            jax.ShapeDtypeStruct((128, RW), F32), jax.ShapeDtypeStruct((128, RW), BF),
            pltpu.VMEM((RW, DEPTH), BF), pltpu.VMEM((RW, DEPTH), BF),
        ),
        in_specs=[vmem] * 16,
        out_specs=(vmem,) * 4,
        scratch_shapes=[
            pltpu.VMEM((GROUPS * PAY, 128), BF),
            pltpu.VMEM((NAO, 512), BF),
            pltpu.VMEM((GROUPS, 128), jnp.int32),
            pltpu.SMEM((GROUPS, 128), jnp.int32),
            pltpu.SemaphoreType.DMA((1,)),
        ],
        compiler_params=pltpu.CompilerParams(vmem_limit_bytes=20 * 1024 * 1024),
        cost_estimate=pl.CostEstimate(flops=8 * 10**9, bytes_accessed=8 * 2**20, transcendentals=0),
    )(*tiles, *parts)
    got = swap_core(send)
    send_rest = pl.pallas_call(
        send_kernel,
        out_shape=jax.ShapeDtypeStruct((KEEP_ROW - SEND_ROW, RW), BF),
        in_specs=[vmem] * 2,
        out_specs=vmem,
        compiler_params=limits,
        cost_estimate=cost,
    )(occ, vir)
    ahead, behind = pl.pallas_call(
        first_kernel,
        out_shape=(jax.ShapeDtypeStruct((64, RW), BF),) * 2,
        in_specs=[vmem, vmem, pl.BlockSpec(memory_space=pl.ANY)],
        out_specs=(vmem,) * 2,
        compiler_params=limits,
    )(keep, got, send_rest)
    send_rest, ahead = lax.optimization_barrier((send_rest, ahead))
    keeps = pl.pallas_call(
        keep_kernel,
        out_shape=(jax.ShapeDtypeStruct((128, RW), F32),) * 3,
        in_specs=[vmem, vmem, pl.BlockSpec(memory_space=pl.ANY)],
        out_specs=(vmem,) * 3,
        compiler_params=limits,
        cost_estimate=cost,
    )(occ, vir, ahead)
    return along_y(ahead, 1), along_y(behind, -1), swap_core(send_rest), keeps


def gather_tiles(payload):
    across = swap_x(payload)
    east, west = along_y(payload, 1), along_y(payload, -1)
    east_across, west_across = along_y(across, 1), along_y(across, -1)
    return payload, across, east, west, east_across, west_across, along_y(east, 1), along_y(west_across, -1)


def gather_green(pieces):
    first = permute(pieces, scatter_target)
    above, below = along_z(first, -1), along_z(first, 1)
    parts = (first, above, below, along_z(below, 1))
    return parts + tuple(swap_core(part) for part in parts)


def reduce_band(ahead, behind, got, keeps):
    own, one, three = [
        keep + got[number * 128:(number + 1) * 128].astype(F32) for number, keep in enumerate(keeps)
    ]
    up = jnp.concatenate([one[:64] + ahead.astype(F32), one[64:]], axis=0).astype(BF)
    down = jnp.concatenate([three[:64], three[64:] + behind.astype(F32)], axis=0).astype(BF)
    up, down = along_y(up, 1), along_y(down, -1)
    total = own + up.astype(F32) + down.astype(F32)
    upper = total[:32] + swap_x(total[64:96].astype(BF)).astype(F32)
    lower = next_group(total[32:64].astype(BF), 0).astype(F32) + next_group(total[96:].astype(BF), 1).astype(F32)
    return jnp.concatenate([lower[:, :512], lower[:, 512:] + upper[:, :512], upper[:, 512:]], axis=1)


def per_device(green_occ, green_virtual, tile_values, tile_orbital, tile_window, tile_count):
    pieces = cut_pieces(green_occ, green_virtual)
    payload = pack(tile_orbital, tile_window, tile_count, tile_values, pieces)
    tiles, parts = gather_tiles(payload), gather_green(pieces)
    return reduce_band(*chi_call(tiles, parts))


def solution(mesh):
    in_specs = (
        P(None, "ao"),
        P(None, "ao"),
        P(("ao", "pair"), None, None),
        P(("ao", "pair")),
        P(("ao", "pair")),
        P(("ao", "pair")),
    )
    out_specs = P(("ao", "pair"), None)
    return jax.shard_map(
        per_device, mesh=mesh, in_specs=in_specs, out_specs=out_specs, check_vma=False
    )
```

```python
import functools

import jax
import jax.numpy as jnp
from jax import lax
from jax.experimental import pallas as pl
from jax.experimental.pallas import tpu as pltpu
from jax.sharding import PartitionSpec as P

AXES = ("ao", "pair")
BLK = 64
TILES = 16
PAIRS = TILES // 2
NAO = 2048
RW = 1024
COLS = 128
PIECE = NAO // 8
META = 16
BODY = PAIRS * 128
PAY = BODY + META
GROUPS = 8
DEPTH = GROUPS * 512
BF = jnp.bfloat16
F32 = jnp.float32


def device_of(index):
    ao, pair = index // 16, index % 16
    return ao // 8, ao % 8, pair // 4, (pair // 2) % 2, pair % 2


def index_of(x_hi, z, y, x_lo, core):
    return ((x_hi % 2) * 8 + z % 8) * 16 + ((y % 4) * 2 + x_lo % 2) * 2 + core % 2


def permute(value, where):
    pairs = [(source, index_of(*where(*device_of(source)))) for source in range(256)]
    return lax.ppermute(value, AXES, pairs)


def along_y(value, steps):
    return permute(value, lambda x_hi, z, y, x_lo, core: (x_hi, z, y + steps, x_lo, core))


def along_z(value, steps):
    return permute(value, lambda x_hi, z, y, x_lo, core: (x_hi, z + steps, y, x_lo, core))


def swap_x(value):
    return permute(value, lambda x_hi, z, y, x_lo, core: (x_hi, z, y, x_lo + 1, core))


def swap_core(value):
    return permute(value, lambda x_hi, z, y, x_lo, core: (x_hi, z, y, x_lo, core + 1))


def next_group(value, flip):
    def where(x_hi, z, y, x_lo, core):
        return (x_hi + (z == 7), z + 1, y, x_lo + flip, core)

    return permute(value, where)


Z_OFFSETS = (3, 6, 1, 5, 7, 0, 4, 2)


def scatter_target(x_hi, z, y, x_lo, core):
    target_y, target_x, target_core = z % 4, x_hi, z // 4
    target_hi = x_hi + (x_lo - target_x) % 2
    return target_hi, z + Z_OFFSETS[(y - target_y) % 4 * 2 + core], target_y, target_x, target_core


def piece_copies(occ_ref, vir_ref, out_ref, sems):
    ao, pair = lax.axis_index("ao"), lax.axis_index("pair")
    z, y, core = lax.rem(ao, 8), pair // 4, lax.rem(pair, 2)
    case = lax.rem(y - lax.rem(z, 4) + 4, 4) * 2 + core
    target_z = z
    for number, offset in enumerate(Z_OFFSETS):
        target_z = target_z + jnp.where(case == number, offset, 0)
    copies = []
    for spot in range(2):
        start = pl.multiple_of(lax.rem(target_z + 4 * spot, 8) * PIECE, PIECE)
        for part, ref in enumerate((occ_ref, vir_ref)):
            copies.append(pltpu.make_async_copy(
                ref.at[pl.ds(start, PIECE)],
                out_ref.at[pl.ds(spot * PIECE, PIECE), pl.ds(part * COLS, COLS)],
                sems.at[spot * 2 + part],
            ))
    return copies


def cut_kernel(occ_ref, vir_ref, piece_ref, sems):
    copies = piece_copies(occ_ref, vir_ref, piece_ref, sems)
    for copy in copies:
        copy.start()
    for copy in copies:
        copy.wait()


def cut_pieces(green_occ, green_virtual):
    return pl.pallas_call(
        cut_kernel,
        out_shape=jax.ShapeDtypeStruct((2 * PIECE, 2 * COLS), BF),
        in_specs=[pl.BlockSpec(memory_space=pl.ANY)] * 2,
        out_specs=pl.BlockSpec(memory_space=pltpu.VMEM),
        scratch_shapes=[pltpu.SemaphoreType.DMA((4,))],
    )(green_occ, green_virtual)


def pack_kernel(orbital_ref, window_ref, count_ref, tile_ref, unused_ref, out_ref, order_ref):
    live = count_ref[0]
    windows = [window_ref[slot] for slot in range(TILES)]
    keys = [
        jnp.where(slot < live, windows[slot], TILES) * TILES + slot for slot in range(TILES)
    ]
    ranks = [jnp.int32(0) for slot in range(TILES)]
    for first in range(TILES):
        for second in range(first + 1, TILES):
            later = (keys[second] < keys[first]).astype(jnp.int32)
            ranks[first] = ranks[first] + later
            ranks[second] = ranks[second] + (1 - later)
    for slot in range(TILES):
        order_ref[ranks[slot]] = slot
    lane = lax.broadcasted_iota(jnp.int32, (META, 128), 1)
    meta = jnp.where(lane == 32, live, jnp.zeros((META, 128), jnp.int32))
    last = jnp.int32(0)
    for slot in range(TILES):
        source = order_ref[slot]
        last = jnp.where(slot < live, window_ref[source], last)
        meta = jnp.where(lane == slot, last, meta)
        meta = jnp.where(lane == TILES + slot, orbital_ref[source], meta)
    for index in range(PAIRS):
        rows = []
        for slot in (2 * index, 2 * index + 1):
            rows.append(jnp.where(slot < live, tile_ref[order_ref[slot]].astype(F32), 0.0))
        both = jnp.concatenate(rows, axis=0)
        out_ref[pl.ds(index * 128, 128), :] = both.T.astype(BF)
    out_ref[pl.ds(BODY, META), :] = meta.astype(F32).astype(BF)


def pack(tile_orbital, tile_window, tile_count, tile_values, pieces):
    smem = pl.BlockSpec(memory_space=pltpu.SMEM)
    vmem = pl.BlockSpec(memory_space=pltpu.VMEM)
    return pl.pallas_call(
        pack_kernel,
        out_shape=pltpu.VMEM((PAY, 128), BF),
        in_specs=[smem, smem, smem, vmem, pl.BlockSpec(memory_space=pl.ANY)],
        out_specs=vmem,
        scratch_shapes=[pltpu.SMEM((TILES,), jnp.int32)],
    )(tile_orbital, tile_window, tile_count, tile_values, pieces)


SEND_ROW, KEEP_ROW = 256, 640
PART_OFFSETS = ((0, 4), (1, 5), (7, 3), (6, 2))


def chi_kernel(*refs):
    tile_parts, green_parts = refs[:8], refs[8:16]
    keep_ref, send_ref, occ_ref, vir_ref = refs[16:20]
    tiles_ref, green_ref, flat_ref, meta_ref, sems = refs[20:]
    ao, pair = lax.axis_index("ao"), lax.axis_index("pair")
    my_z, my_y, my_x, my_core = lax.rem(ao, 8), pair // 4, lax.rem(pair // 2, 2), lax.rem(pair, 2)

    for number, ref in enumerate(tile_parts):
        tiles_ref[pl.ds(number * PAY, PAY), :] = ref[...]
        head = ref[pl.ds(BODY, META), :].astype(F32).astype(jnp.int32)
        flat_ref[pl.ds(number, 1), :] = head[:1]
    to_scalars = pltpu.make_async_copy(flat_ref, meta_ref, sems.at[0])
    to_scalars.start()
    for number, ref in enumerate(green_parts):
        for spot, offset in enumerate(PART_OFFSETS[number % 4]):
            start = pl.multiple_of(lax.rem(my_z + offset, 8) * PIECE, PIECE)
            lanes = number // 4 * 256
            green_ref[pl.ds(start, PIECE), lanes:lanes + 256] = ref[spot * PIECE:(spot + 1) * PIECE, :]
    occ_ref[...] = jnp.zeros_like(occ_ref)
    vir_ref[...] = jnp.zeros_like(vir_ref)
    to_scalars.wait()

    def rows_of(orbital):
        return green_ref[pl.ds(pl.multiple_of(orbital * BLK, BLK), BLK), :]

    def store(block, window, column):
        high, y, x = window // 8, lax.rem(window // 2, 4), lax.rem(window, 2)
        dy, dx = lax.rem(y - my_y + 4, 4), lax.rem(x - my_x + 2, 2)
        spot = (dx * 2 + high) * 32
        far = dy == 2
        rest = jnp.where(dy == 3, 256, dy * 128)
        vir_row = pl.multiple_of(window * BLK, BLK)
        for i in range(2):
            part = block[i * BLK:(i + 1) * BLK]
            occ = jnp.concatenate([part[:, 0:128], part[:, 256:384]], axis=1)
            vir = jnp.concatenate([part[:, 128:256], part[:, 384:512]], axis=1)
            vir_ref[pl.ds(vir_row, BLK), pl.ds(column + i * 256, 256)] = vir
            for core in range(2):
                row = jnp.where(
                    my_core == core, jnp.where(far, 0, KEEP_ROW + rest), jnp.where(far, 128, SEND_ROW + rest)
                )
                row = pl.multiple_of(row + spot, 32)
                occ_ref[pl.ds(row, 32), pl.ds(column + i * 256, 256)] = occ[core * 32:(core + 1) * 32]

    lane = lax.broadcasted_iota(jnp.int32, (1, 128), 1)
    low = jnp.where(lane < BLK, 1.0, 0.0).astype(BF)
    high = jnp.where(lane < BLK, 0.0, 1.0).astype(BF)
    blank = jnp.zeros((128, 128), BF)

    def slots_of(base, number, quads):
        column = pl.multiple_of(number * 512, 512)
        total = None
        for quad in range(quads):
            pair = [
                tiles_ref[pl.ds(pl.multiple_of(base + quad * 256 + k * 128, 16), 128), :] for k in range(2)
            ]
            stacked = jnp.concatenate([
                jnp.concatenate([pair[0] * low, blank], axis=1),
                jnp.concatenate([pair[0] * high, blank], axis=1),
                jnp.concatenate([blank, pair[1] * low], axis=1),
                jnp.concatenate([blank, pair[1] * high], axis=1),
            ], axis=0)
            slots = [4 * quad + t for t in range(4)]
            rows = jnp.concatenate([rows_of(meta_ref[number, TILES + slot]) for slot in slots], axis=0)
            product = jnp.dot(stacked, rows, preferred_element_type=F32)
            for t, slot in enumerate(slots):
                window = meta_ref[number, slot]
                fresh = product[t * 128:(t + 1) * 128]
                if total is None:
                    total = fresh
                else:
                    total = fresh + jnp.where(window == meta_ref[number, slot - 1], total, 0.0)
                store(total.astype(BF), window, column)

    @pl.loop(0, GROUPS)
    def _(number):
        base = number * PAY
        live = meta_ref[number, 2 * TILES]

        for quads in range(1, TILES // 4 + 1):
            @pl.when((live > 4 * quads - 4) & (live <= 4 * quads))
            def _(quads=quads):
                slots_of(base, number, quads)

    product = chi_rows(occ_ref, vir_ref, 0, SEND_ROW)
    keep_ref[...] = product[:128]
    send_ref[...] = product[128:].astype(BF)


def chi_rows(occ_ref, vir_ref, row, rows):
    return lax.dot_general(
        occ_ref[pl.ds(row, rows), :], vir_ref[...], (((1,), (1,)), ((), ())), preferred_element_type=F32
    )


def send_kernel(occ_ref, vir_ref, send_ref):
    send_ref[...] = chi_rows(occ_ref, vir_ref, SEND_ROW, KEEP_ROW - SEND_ROW).astype(BF)


def first_kernel(keep_ref, got_ref, unused_ref, ahead_ref, behind_ref):
    total = keep_ref[...] + got_ref[...].astype(F32)
    ahead_ref[...] = total[:64].astype(BF)
    behind_ref[...] = total[64:].astype(BF)


def keep_kernel(occ_ref, vir_ref, unused_ref, *keep_refs):
    product = chi_rows(occ_ref, vir_ref, KEEP_ROW, RW - KEEP_ROW)
    for number, keep_ref in enumerate(keep_refs):
        keep_ref[...] = product[number * 128:(number + 1) * 128]


def chi_call(tiles, parts):
    vmem = pl.BlockSpec(memory_space=pltpu.VMEM)
    limits = pltpu.CompilerParams(vmem_limit_bytes=12 * 1024 * 1024)
    cost = pl.CostEstimate(flops=4 * 10**9, bytes_accessed=4 * 2**20, transcendentals=0)
    keep, send, occ, vir = pl.pallas_call(
        chi_kernel,
        out_shape=(
            jax.ShapeDtypeStruct((128, RW), F32), jax.ShapeDtypeStruct((128, RW), BF),
            pltpu.VMEM((RW, DEPTH), BF), pltpu.VMEM((RW, DEPTH), BF),
        ),
        in_specs=[vmem] * 16,
        out_specs=(vmem,) * 4,
        scratch_shapes=[
            pltpu.VMEM((GROUPS * PAY, 128), BF),
            pltpu.VMEM((NAO, 512), BF),
            pltpu.VMEM((GROUPS, 128), jnp.int32),
            pltpu.SMEM((GROUPS, 128), jnp.int32),
            pltpu.SemaphoreType.DMA((1,)),
        ],
        compiler_params=pltpu.CompilerParams(vmem_limit_bytes=20 * 1024 * 1024),
        cost_estimate=pl.CostEstimate(flops=8 * 10**9, bytes_accessed=8 * 2**20, transcendentals=0),
    )(*tiles, *parts)
    got = swap_core(send)
    send_rest = pl.pallas_call(
        send_kernel,
        out_shape=jax.ShapeDtypeStruct((KEEP_ROW - SEND_ROW, RW), BF),
        in_specs=[vmem] * 2,
        out_specs=vmem,
        compiler_params=limits,
        cost_estimate=cost,
    )(occ, vir)
    ahead, behind = pl.pallas_call(
        first_kernel,
        out_shape=(jax.ShapeDtypeStruct((64, RW), BF),) * 2,
        in_specs=[vmem, vmem, pl.BlockSpec(memory_space=pl.ANY)],
        out_specs=(vmem,) * 2,
        compiler_params=limits,
    )(keep, got, send_rest)
    send_rest, ahead = lax.optimization_barrier((send_rest, ahead))
    keeps = pl.pallas_call(
        keep_kernel,
        out_shape=(jax.ShapeDtypeStruct((128, RW), F32),) * 3,
        in_specs=[vmem, vmem, pl.BlockSpec(memory_space=pl.ANY)],
        out_specs=(vmem,) * 3,
        compiler_params=limits,
        cost_estimate=cost,
    )(occ, vir, ahead)
    return along_y(ahead, 1), along_y(behind, -1), swap_core(send_rest), keeps


def gather_tiles(payload):
    across = swap_x(payload)
    east, west = along_y(payload, 1), along_y(payload, -1)
    east_across, west_across = along_y(across, 1), along_y(across, -1)
    return payload, across, east, west, east_across, west_across, along_y(east, 1), along_y(west_across, -1)


def gather_green(pieces):
    first = permute(pieces, scatter_target)
    above, below = along_z(first, -1), along_z(first, 1)
    parts = (first, above, below, along_z(below, 1))
    return parts + tuple(swap_core(part) for part in parts)


def reduce_band(ahead, behind, got, keeps):
    own, one, three = [
        keep + got[number * 128:(number + 1) * 128].astype(F32) for number, keep in enumerate(keeps)
    ]
    up = jnp.concatenate([one[:64] + ahead.astype(F32), one[64:]], axis=0).astype(BF)
    down = jnp.concatenate([three[:64], three[64:] + behind.astype(F32)], axis=0).astype(BF)
    up, down = along_y(up, 1), along_y(down, -1)
    total = own + up.astype(F32) + down.astype(F32)
    upper = total[:32] + swap_x(total[64:96].astype(BF)).astype(F32)
    lower = next_group(total[32:64].astype(BF), 0).astype(F32) + next_group(total[96:].astype(BF), 1).astype(F32)
    return jnp.concatenate([lower[:, :512], lower[:, 512:] + upper[:, :512], upper[:, 512:]], axis=1)


def per_device(green_occ, green_virtual, tile_values, tile_orbital, tile_window, tile_count):
    pieces = cut_pieces(green_occ, green_virtual)
    payload = pack(tile_orbital, tile_window, tile_count, tile_values, pieces)
    tiles, parts = gather_tiles(payload), gather_green(pieces)
    return reduce_band(*chi_call(tiles, parts))


def solution(mesh):
    in_specs = (
        P(None, "ao"),
        P(None, "ao"),
        P(("ao", "pair"), None, None),
        P(("ao", "pair")),
        P(("ao", "pair")),
        P(("ao", "pair")),
    )
    out_specs = P(("ao", "pair"), None)
    return jax.shard_map(
        per_device, mesh=mesh, in_specs=in_specs, out_specs=out_specs, check_vma=False
    )
```
